128 devices in a mesh: gx: 4 (over y_hi, core), gy: 32 (over x, z, y_lo).
Axes of the slice: x: 4, y: 4 (y_hi: 2, y_lo: 2; y = y_hi * 2 + y_lo), z: 4, core: 2. Of those that a mesh axis runs over, the one named last changes fastest.
Arguments:
- right_side: float32 [32, 256, 128, 128], P('gx', 'gy'), may hold values from -6 to 6
- diag_blocks: float32 [32, 256, 128, 128], P('gx', 'gy'), as said below
- smoother: float32 [32, 256, 128, 128], P('gx', 'gy'), as said below
- face_weight: float32 [32, 256, 4, 128], P('gx', 'gy'), may hold values from 0.3 to 1.5
- restrict_weight: float32 [32, 256, 128], P('gx', 'gy'), may hold values from 0.2 to 1
- prolong_weight: float32 [32, 256, 128], P('gx', 'gy'), may hold values from 0.3 to 1.2
- block_owner: int32 [32, 256], P('gx', 'gy'), may hold values from 0 to 31, as said below
- block_aggregate: int32 [32, 256], P('gx', 'gy'), may hold values from 0 to 31, as said below
- coarse_diag: float32 [1024, 128, 128], P('gy'), as said below
- coarse_smooth: float32 [1024, 128, 128], P('gy'), as said below
- neighbors: int32 [1024, 6], P('gy'), may hold values from 0 to 1023, as said below
- neighbor_weight: float32 [1024, 6, 128], P('gy'), may hold values from 0.2 to 1
Outputs:
- solution: float32 [32, 256, 128, 128], P('gx', 'gy')
- fine_residual: float32 [32, 256, 128, 128], P('gx', 'gy')
The draws below stay inside these ranges and needn't reach their ends.
Inputs may be any that keep to these rules, and one draw needn't show every extreme that they name: block_owner[p,q] differs from q // 8 by at most one. Within one device's blocks, 1 to 16 name the lower neighbouring owner and 1 to 16 the upper one (none beyond the ends of gy), and for every index of gy some device sends exactly 16 each way that exists. block_aggregate[p,q] differs from p * 1 by at most one. neighbors[a,n] // 32 differs from a // 32 by at most one. `diag_blocks`: each matrix has its diagonal between 4 and 8 and off-diagonal entries within 0.2 in magnitude. `smoother`: each matrix has its diagonal between 0.12 and 0.25 and off-diagonal entries within 0.006 in magnitude. `coarse_diag`: each matrix has its diagonal between 4 and 8 and off-diagonal entries within 0.2 in magnitude. `coarse_smooth`: each matrix has its diagonal between 0.12 and 0.25 and off-diagonal entries within 0.006 in magnitude.
All inputs are finite; a program needn't handle non-finite values.
Results may differ from the reference program's by a relative error of at most 0.000073.
Values sent between devices are 32-bit elements; how exact they have to be, the bound alone decides.
No kernel may reach another device: no remote copies, remote signals or barrier semaphores. Data moves between devices by JAX's collectives and lax.ppermute only.
A program may use at most 320 MiB of HBM per device.

```python
import math
import jax
import jax.numpy as jnp
from jax import lax

BS = 128
BX = 8
BY = 8
K = 128
AGG_DEV = 32
NBR = 6
NBX = 32
NBY = 256
NAGG = 1024
CAP = 16
N_GX = 4
N_GY = 32


def blend(diagonal, off_diag):
    identity = jnp.eye(off_diag.shape[-1], dtype=jnp.float32)
    return off_diag * (1.0 - identity) + identity * diagonal[..., :, None]


def dominant(key, leading, lower, upper, spread):
    first_key, second_key = jax.random.split(key)
    diagonal = jax.random.uniform(first_key, leading + (BS,), jnp.float32, lower, upper)
    off_diag = jax.random.uniform(second_key, leading + (BS, BS), jnp.float32, -spread, spread)
    return blend(diagonal, off_diag)


def draw_diag_blocks(key, part):
    key = jax.random.fold_in(key, 3)
    return dominant(key, (NBX, NBY), 4.0, 8.0, 0.2)


def draw_smoother(key, part):
    key = jax.random.fold_in(key, 5)
    return dominant(key, (NBX, NBY), 0.12, 0.25, 0.006)


def draw_coarse_diag(key, part):
    key = jax.random.fold_in(key, 9)
    return dominant(key, (NAGG,), 4.0, 8.0, 0.2)


def draw_coarse_smooth(key, part):
    key = jax.random.fold_in(key, 17)
    return dominant(key, (NAGG,), 0.12, 0.25, 0.006)


def draw_block_owner(key, part):
    key = jax.random.fold_in(key, 7)
    hot_key, lower_key, upper_key = jax.random.split(key, 3)
    hot_row = jax.random.randint(hot_key, (N_GY,), 0, N_GX)
    lower_count = jax.random.randint(lower_key, (N_GX, N_GY), 1, CAP + 1)
    upper_count = jax.random.randint(upper_key, (N_GX, N_GY), 1, CAP + 1)
    hot_tile = jnp.arange(N_GX, dtype=jnp.int32)[:, None] == hot_row[None, :]
    lower_count = jnp.where(hot_tile, CAP, lower_count)
    upper_count = jnp.where(hot_tile, CAP, upper_count)
    column_index = jnp.arange(N_GY, dtype=jnp.int32)[None, :]
    lower_count = jnp.where(column_index == 0, 0, lower_count)
    upper_count = jnp.where(column_index == N_GY - 1, 0, upper_count)
    rows = jnp.arange(NBX, dtype=jnp.int32)[:, None]
    cols = jnp.arange(NBY, dtype=jnp.int32)[None, :]
    tile_x = jnp.broadcast_to(rows // BX, (NBX, NBY))
    home = jnp.broadcast_to(cols // BY, (NBX, NBY))
    order = cols % BY * BX + rows % BX
    lower_here = lower_count[tile_x, home]
    upper_here = upper_count[tile_x, home]
    owner = jnp.where(order < lower_here, home - 1, jnp.where(order >= BX * BY - upper_here, home + 1, home))
    return owner.astype(jnp.int32)


def draw_block_aggregate(key, part):
    key = jax.random.fold_in(key, 11)
    jitter = jax.random.randint(key, (NBX, NBY), -1, 2)
    rows = jnp.arange(NBX, dtype=jnp.int32)[:, None]
    return jnp.clip((rows + jitter) * AGG_DEV // NBX, 0, AGG_DEV - 1).astype(jnp.int32)


def draw_neighbors(key, part):
    key = jax.random.fold_in(key, 13)
    owners = jnp.arange(NAGG, dtype=jnp.int32) // AGG_DEV
    lower = jnp.maximum(owners - 1, 0) * AGG_DEV
    upper = jnp.minimum(owners + 2, N_GY) * AGG_DEV
    raw = jax.random.randint(key, (NAGG, NBR), 0, 2 ** 20)
    return (lower[:, None] + raw % (upper - lower)[:, None]).astype(jnp.int32)


def level_of(own_key, shape, cuts, least, high):
    factor_of, own = 1.0, jax.random.fold_in(own_key, 6)
    for axis_at, parts in cuts:
        draws = jnp.exp(jax.random.uniform(jax.random.fold_in(own, axis_at), (parts,), jnp.float32, least / len(cuts), high / len(cuts)))
        factor_of = factor_of * jnp.repeat(draws, shape[axis_at] // parts).reshape([-1 if axis == axis_at else 1 for axis in range(len(shape))])
    return factor_of


def scatter_about(key, dims, scale, bound, pieces=(), kind=jnp.bfloat16):
    entries = jax.random.normal(key, dims, jnp.float32) * scale
    if len(pieces) > 0:
        entries = level_of(key, dims, pieces, -0.22, 0.18) * entries
    return jnp.clip(entries, min=-bound, max=bound).astype(kind)


def setup_inputs(seed: int = 0) -> dict:
    splits = jax.random.split(jax.random.key(seed), 13)
    right_side = scatter_about(splits[0], (NBX, NBY, K, BS), 1.0, 6.0, ((0, 4), (1, 32)), jnp.float32)
    diag_blocks = draw_diag_blocks(jax.random.fold_in(splits[12], 71), 0)
    smoother = draw_smoother(jax.random.fold_in(splits[12], 71), 0)
    face_weight = jnp.clip(jnp.exp(math.log(1.5) - 1.60943787 * jax.random.uniform(splits[3], (NBX, NBY, 4, BS), jnp.float32) ** level_of(splits[3], (NBX, NBY, 4, BS), ((0, 4), (1, 32)), -0.2, 0.2)), 0.3, 1.5)
    restrict_weight = jnp.clip(0.2 + 0.8 * jax.random.uniform(splits[4], (NBX, NBY, BS), jnp.float32) ** level_of(splits[4], (NBX, NBY, BS), ((0, 4), (1, 32)), -0.2, 0.2), 0.2, 1.0)
    prolong_weight = jnp.clip(0.3 + 0.90000004 * jax.random.uniform(splits[5], (NBX, NBY, BS), jnp.float32) ** level_of(splits[5], (NBX, NBY, BS), ((0, 4), (1, 32)), -0.2, 0.2), 0.3, 1.2)
    block_owner = draw_block_owner(jax.random.fold_in(splits[12], 71), 0)
    block_aggregate = draw_block_aggregate(jax.random.fold_in(splits[12], 71), 0)
    coarse_diag = draw_coarse_diag(jax.random.fold_in(splits[12], 71), 0)
    coarse_smooth = draw_coarse_smooth(jax.random.fold_in(splits[12], 71), 0)
    neighbors = draw_neighbors(jax.random.fold_in(splits[12], 71), 0)
    neighbor_weight = jnp.clip(jnp.exp(math.log(1.0) - 1.609438 * jax.random.uniform(splits[11], (NAGG, NBR, BS), jnp.float32) ** level_of(splits[11], (NAGG, NBR, BS), ((0, 32),), -0.2, 0.2)), 0.2, 1.0)
    return {"right_side": right_side, "diag_blocks": diag_blocks, "smoother": smoother, "face_weight": face_weight, "restrict_weight": restrict_weight, "prolong_weight": prolong_weight, "block_owner": block_owner, "block_aggregate": block_aggregate, "coarse_diag": coarse_diag, "coarse_smooth": coarse_smooth, "neighbors": neighbors, "neighbor_weight": neighbor_weight}


HIGHEST = lax.Precision.HIGHEST


def apply_blocks(matrices, vector):
    return jnp.einsum('...ij,...kj->...ki', matrices, vector, precision=HIGHEST)


def fine_apply(vector, diag_blocks, face_weight):
    padded = jnp.pad(vector, ((1, 1), (1, 1), (0, 0), (0, 0)))
    result = apply_blocks(diag_blocks, vector)
    result = result - face_weight[:, :, 0, None, :] * padded[:-2, 1:-1]
    result = result - face_weight[:, :, 1, None, :] * padded[2:, 1:-1]
    result = result - face_weight[:, :, 2, None, :] * padded[1:-1, :-2]
    result = result - face_weight[:, :, 3, None, :] * padded[1:-1, 2:]
    return result


def reference(right_side, diag_blocks, smoother, face_weight, restrict_weight, prolong_weight, block_owner, block_aggregate, coarse_diag, coarse_smooth, neighbors, neighbor_weight):
    first_sweep = apply_blocks(smoother, right_side)
    fine_part = first_sweep + apply_blocks(smoother, right_side - fine_apply(first_sweep, diag_blocks, face_weight))
    aggregate_ids = (block_owner * AGG_DEV + block_aggregate).astype(jnp.int32).reshape(-1)
    weighted = (restrict_weight[:, :, None, :] * right_side).reshape(NBX * NBY, K, BS)
    coarse_rhs = jax.ops.segment_sum(weighted, aggregate_ids, num_segments=NAGG)
    coarse_first = apply_blocks(coarse_smooth, coarse_rhs)
    gathered = coarse_first[neighbors.astype(jnp.int32)]
    coupling = jnp.sum(neighbor_weight[:, :, None, :] * gathered, axis=1)
    image = apply_blocks(coarse_diag, coarse_first) - coupling
    coarse_corr = coarse_first + apply_blocks(coarse_smooth, coarse_rhs - image)
    spread = coarse_corr[aggregate_ids].reshape(NBX, NBY, K, BS)
    solution = fine_part + prolong_weight[:, :, None, :] * spread
    fine_residual = right_side - fine_apply(solution, diag_blocks, face_weight)
    return solution, fine_residual
```

```python
import functools

import jax
import jax.numpy as jnp
from jax import lax
from jax.experimental import pallas as pl
from jax.experimental.pallas import tpu as pltpu
from jax.sharding import PartitionSpec as P

F32 = jnp.float32
BF16 = jnp.bfloat16
VMEM_LIMIT = 40 * 1024 * 1024


def shifted(array, axis, by):
    size = lax.axis_size(axis)
    pairs = [(i, i + by) for i in range(size) if 0 <= i + by < size]
    return lax.ppermute(array, axis, pairs)


def halves(x):
    high = x.astype(BF16)
    low = (x - high.astype(F32)).astype(BF16)
    return high, low


def product(vector, matrix):
    vector_high, vector_low = halves(vector)
    matrix_high, matrix_low = halves(matrix)
    left = jnp.concatenate([vector_high, vector_low], axis=1)
    right = jnp.concatenate(
        [
            jnp.concatenate([matrix_high, matrix_high], axis=1),
            jnp.concatenate([matrix_low, matrix_low], axis=1),
        ],
        axis=0,
    )
    both = lax.dot_general(left, right, (((1,), (1,)), ((), ())), preferred_element_type=F32)
    width = matrix.shape[0]
    return both[:, :width] + both[:, width:]


def call(kernel, grid, in_specs, out_specs, out_shape, scalars=0, scratch=(), flops=0, moved=0):
    return pl.pallas_call(
        kernel,
        grid_spec=pltpu.PrefetchScalarGridSpec(
            num_scalar_prefetch=scalars,
            grid=(grid,),
            in_specs=in_specs,
            out_specs=out_specs,
            scratch_shapes=list(scratch),
        ),
        out_shape=out_shape,
        compiler_params=pltpu.CompilerParams(vmem_limit_bytes=VMEM_LIMIT),
        cost_estimate=pl.CostEstimate(flops=flops, bytes_accessed=moved, transcendentals=0),
    )


def step_block(shape):
    return pl.BlockSpec((1,) + tuple(shape[1:]), lambda s, *_: (s,) + (0,) * (len(shape) - 1))


def part_block(shape, count):
    return pl.BlockSpec((count,) + tuple(shape[1:]), lambda s, *_: (s,) + (0,) * (len(shape) - 1))


def whole(shape):
    return pl.BlockSpec(tuple(shape), lambda s, *_: (0,) * len(shape))


def like(shape):
    return jax.ShapeDtypeStruct(tuple(shape), F32)


def restrict_kernel(parts, pos, owner, agg, r_ref, w_ref, low_ref, own_ref, up_ref, acc):
    s = pl.program_id(0)
    last = pl.num_programs(0) - 1
    blocks_y = r_ref.shape[1]

    @pl.when(s == 0)
    def _():
        acc[...] = jnp.zeros_like(acc)

    for b in range(blocks_y):
        side = owner[s, b] - pos[1] + 1
        slot = agg[s, b] - pos[0] + 1
        acc[side, slot] += w_ref[0, b][None, :] * r_ref[0, b]

    @pl.when(s == last)
    def _():
        rows = acc.shape[2] // parts
        for side, ref in ((0, low_ref), (1, own_ref), (2, up_ref)):
            for part in range(parts):
                ref[part] = acc[side, :, part * rows : (part + 1) * rows]


def put_faces(s, last, row_ref, x_first, x_last, y_first, y_last):
    y_first[0] = row_ref[0, 0]
    y_last[0] = row_ref[0, row_ref.shape[1] - 1]

    @pl.when(s == 0)
    def _():
        x_first[...] = row_ref[0]

    @pl.when(s == last)
    def _():
        x_last[...] = row_ref[0]


def sweep_kernel(r_ref, s_ref, f_ref, x_first, x_last, y_first, y_last):
    s = pl.program_id(0)
    for b in range(r_ref.shape[1]):
        f_ref[0, b] = product(r_ref[0, b], s_ref[0, b])
    put_faces(s, pl.num_programs(0) - 1, f_ref, x_first, x_last, y_first, y_last)


def operator_row(s, v_ref, diag_ref, face_ref, x_low, x_high, y_low, y_high, before, after):
    last = pl.num_programs(0) - 1
    blocks_y = v_ref.shape[1]

    @pl.when(s == 0)
    def _():
        before[...] = x_low[...]

    @pl.when(s > 0)
    def _():
        before[...] = v_ref[jnp.maximum(s - 1, 0)]

    @pl.when(s == last)
    def _():
        after[...] = x_high[...]

    @pl.when(s < last)
    def _():
        after[...] = v_ref[jnp.minimum(s + 1, last)]

    for b in range(blocks_y):
        here = v_ref[s, b]
        left = y_low[0] if b == 0 else v_ref[s, b - 1]
        right = y_high[0] if b == blocks_y - 1 else v_ref[s, b + 1]
        result = product(here, diag_ref[0, b])
        result = result - face_ref[0, b, 0][None, :] * before[b]
        result = result - face_ref[0, b, 1][None, :] * after[b]
        result = result - face_ref[0, b, 2][None, :] * left
        result = result - face_ref[0, b, 3][None, :] * right
        yield b, here, result


def fine_kernel(
    r_ref, s_ref, diag_ref, face_ref, v_ref, x_low, x_high, y_low, y_high, out_ref, before, after
):
    s = pl.program_id(0)
    rows = operator_row(
        s, v_ref, diag_ref, face_ref, x_low, x_high, y_low, y_high, before, after
    )
    for b, here, image in rows:
        out_ref[0, b] = here + product(r_ref[0, b] - image, s_ref[0, b])


def residual_kernel(
    r_ref, diag_ref, face_ref, v_ref, x_low, x_high, y_low, y_high, out_ref, before, after
):
    s = pl.program_id(0)
    rows = operator_row(
        s, v_ref, diag_ref, face_ref, x_low, x_high, y_low, y_high, before, after
    )
    for b, _, image in rows:
        out_ref[0, b] = r_ref[0, b] - image


def coarse_first_kernel(got_ref, smooth_ref, rhs_ref, first_ref):
    s = pl.program_id(0)
    last = pl.num_programs(0) - 1
    count = smooth_ref.shape[0]
    for i in range(count):
        value = got_ref[s, i + 1]
        if i == 0:
            value = value + jnp.where(s > 0, got_ref[jnp.maximum(s - 1, 0), count + 1], 0.0)
        if i == count - 1:
            value = value + jnp.where(s < last, got_ref[jnp.minimum(s + 1, last), 0], 0.0)
        rhs_ref[i] = value
        first_ref[i] = product(value, smooth_ref[i])


def coarse_own_kernel(pos, nbr, rhs_ref, first_ref, diag_ref, weight_ref, out_ref):
    s = pl.program_id(0)
    count = rhs_ref.shape[0]
    total = first_ref.shape[0]
    for i in range(count):
        a = s * count + i
        value = rhs_ref[i] - product(first_ref[a], diag_ref[i])
        for n in range(weight_ref.shape[1]):
            at = nbr[a, n] - pos[1] * total
            mine = (at >= 0) & (at < total)
            at = jnp.clip(at, 0, total - 1)
            value = value + jnp.where(mine, weight_ref[i, n], 0.0)[None, :] * first_ref[at]
        out_ref[i] = value


def coarse_last_kernel(
    pos, nbr, own_ref, first_ref, below_ref, above_ref, smooth_ref, weight_ref, out_ref
):
    s = pl.program_id(0)
    last = pl.num_programs(0) - 1
    count = own_ref.shape[0]
    total = below_ref.shape[0]

    @pl.when(s == 0)
    def _():
        out_ref[0, 0] = jnp.zeros_like(own_ref[0])
        out_ref[last, count + 1] = jnp.zeros_like(own_ref[0])

    for i in range(count):
        a = s * count + i
        value = own_ref[i]
        for n in range(weight_ref.shape[1]):
            at = nbr[a, n] - pos[1] * total
            lower = at < 0
            upper = at >= total
            at_lower = jnp.clip(at + total, 0, total - 1)
            at_upper = jnp.clip(at - total, 0, total - 1)
            weight = weight_ref[i, n]
            value = value + jnp.where(lower, weight, 0.0)[None, :] * below_ref[at_lower]
            value = value + jnp.where(upper, weight, 0.0)[None, :] * above_ref[at_upper]
        value = first_ref[i] + product(value, smooth_ref[i])
        out_ref[s, i + 1] = value
        if i == 0:

            @pl.when(s > 0)
            def _():
                out_ref[jnp.maximum(s - 1, 0), count + 1] = value

        if i == count - 1:

            @pl.when(s < last)
            def _():
                out_ref[jnp.minimum(s + 1, last), 0] = value


def prolong_kernel(
    pos,
    owner,
    agg,
    fine_ref,
    w_ref,
    low_ref,
    own_ref,
    up_ref,
    out_ref,
    x_first,
    x_last,
    y_first,
    y_last,
    table,
):
    s = pl.program_id(0)
    parts, _, rows, _ = own_ref.shape

    @pl.when(s == 0)
    def _():
        for side, ref in ((0, low_ref), (1, own_ref), (2, up_ref)):
            for part in range(parts):
                table[side, :, part * rows : (part + 1) * rows] = ref[part]

    for b in range(fine_ref.shape[1]):
        side = owner[s, b] - pos[1] + 1
        slot = agg[s, b] - pos[0] + 1
        out_ref[0, b] = fine_ref[0, b] + w_ref[0, b][None, :] * table[side, slot]
    put_faces(s, pl.num_programs(0) - 1, out_ref, x_first, x_last, y_first, y_last)


def halo(faces):
    x_first, x_last, y_first, y_last = faces
    y_low = shifted(y_last, "gy", 1)
    y_high = shifted(y_first, "gy", -1)
    x_low = shifted(x_last, "gx", 1)
    x_high = shifted(x_first, "gx", -1)
    return x_low, x_high, y_low, y_high


def body(
    right_side,
    diag_blocks,
    smoother,
    face_weight,
    restrict_weight,
    prolong_weight,
    block_owner,
    block_aggregate,
    coarse_diag,
    coarse_smooth,
    neighbors,
    neighbor_weight,
):
    blocks_x, blocks_y, rows, size = right_side.shape
    total = coarse_diag.shape[0]
    parts = lax.axis_size("gx")
    share = total // parts
    fine_shape = right_side.shape
    mat_shape = diag_blocks.shape
    slab = (parts, share + 2, rows // parts, size)
    coarse_shape = (total, rows // parts, size)
    cmat_shape = coarse_diag.shape
    nw_shape = neighbor_weight.shape
    x_face = (blocks_y, rows, size)
    y_face = (blocks_x, rows, size)
    block_flops = 2 * 4 * rows * size * size
    fine_count = blocks_x * blocks_y
    fine_bytes = fine_count * rows * size * 4
    coarse_flops = total * block_flops // parts
    coarse_bytes = total * size * size * 4

    pos = jnp.stack([lax.axis_index("gx") * share, lax.axis_index("gy")]).astype(jnp.int32)

    low, own, up = call(
        functools.partial(restrict_kernel, parts),
        blocks_x,
        [step_block(fine_shape), step_block(restrict_weight.shape)],
        [whole(slab)] * 3,
        [like(slab)] * 3,
        scalars=3,
        scratch=[pltpu.VMEM((3, share + 2, rows, size), F32)],
        moved=2 * fine_bytes,
    )(pos, block_owner, block_aggregate, right_side, restrict_weight)

    from_above = shifted(low, "gy", -1)
    from_below = shifted(up, "gy", 1)

    face_specs = [whole(x_face), whole(x_face), step_block(y_face), step_block(y_face)]
    face_shapes = [like(x_face), like(x_face), like(y_face), like(y_face)]

    sweep, *faces = call(
        sweep_kernel,
        blocks_x,
        [step_block(fine_shape), step_block(mat_shape)],
        [step_block(fine_shape)] + face_specs,
        [like(fine_shape)] + face_shapes,
        flops=fine_count * block_flops,
        moved=3 * fine_bytes,
    )(right_side, smoother)

    got = lax.all_to_all(own + from_above + from_below, "gx", 0, 0, tiled=True)

    rhs, first = call(
        coarse_first_kernel,
        parts,
        [whole(slab), part_block(cmat_shape, share)],
        [part_block(coarse_shape, share)] * 2,
        [like(coarse_shape)] * 2,
        flops=coarse_flops,
        moved=coarse_bytes,
    )(got, coarse_smooth)

    below = shifted(first, "gy", 1)
    above = shifted(first, "gy", -1)

    inner = call(
        coarse_own_kernel,
        parts,
        [
            part_block(coarse_shape, share),
            whole(coarse_shape),
            part_block(cmat_shape, share),
            part_block(nw_shape, share),
        ],
        part_block(coarse_shape, share),
        like(coarse_shape),
        scalars=2,
        flops=coarse_flops,
        moved=coarse_bytes,
    )(pos, neighbors, rhs, first, coarse_diag, neighbor_weight)

    sweep_halo = halo(faces)
    fine_part = call(
        fine_kernel,
        blocks_x,
        [
            step_block(fine_shape),
            step_block(mat_shape),
            step_block(mat_shape),
            step_block(face_weight.shape),
            whole(fine_shape),
            whole(x_face),
            whole(x_face),
            step_block(y_face),
            step_block(y_face),
        ],
        step_block(fine_shape),
        like(fine_shape),
        scratch=[pltpu.VMEM(x_face, F32)] * 2,
        flops=2 * fine_count * block_flops,
        moved=5 * fine_bytes,
    )(right_side, smoother, diag_blocks, face_weight, sweep, *sweep_halo)

    corr = call(
        coarse_last_kernel,
        parts,
        [
            part_block(coarse_shape, share),
            part_block(coarse_shape, share),
            whole(coarse_shape),
            whole(coarse_shape),
            part_block(cmat_shape, share),
            part_block(nw_shape, share),
        ],
        whole(slab),
        like(slab),
        scalars=2,
        flops=coarse_flops,
        moved=coarse_bytes,
    )(pos, neighbors, inner, first, below, above, coarse_smooth, neighbor_weight)

    mine = lax.all_to_all(corr, "gx", 0, 0, tiled=True)
    lower = shifted(mine, "gy", 1)
    upper = shifted(mine, "gy", -1)

    solved, *faces = call(
        prolong_kernel,
        blocks_x,
        [step_block(fine_shape), step_block(prolong_weight.shape)] + [whole(slab)] * 3,
        [step_block(fine_shape)] + face_specs,
        [like(fine_shape)] + face_shapes,
        scalars=3,
        scratch=[pltpu.VMEM((3, share + 2, rows, size), F32)],
        moved=3 * fine_bytes,
    )(pos, block_owner, block_aggregate, fine_part, prolong_weight, lower, mine, upper)

    solved_halo = halo(faces)
    residual = call(
        residual_kernel,
        blocks_x,
        [
            step_block(fine_shape),
            step_block(mat_shape),
            step_block(face_weight.shape),
            whole(fine_shape),
            whole(x_face),
            whole(x_face),
            step_block(y_face),
            step_block(y_face),
        ],
        step_block(fine_shape),
        like(fine_shape),
        scratch=[pltpu.VMEM(x_face, F32)] * 2,
        flops=fine_count * block_flops,
        moved=4 * fine_bytes,
    )(right_side, diag_blocks, face_weight, solved, *solved_halo)
    return (solved, residual)


def solution(mesh):
    return jax.shard_map(
        body,
        mesh=mesh,
        in_specs=(
            P("gx", "gy", None, None),
            P("gx", "gy", None, None),
            P("gx", "gy", None, None),
            P("gx", "gy", None, None),
            P("gx", "gy", None),
            P("gx", "gy", None),
            P("gx", "gy"),
            P("gx", "gy"),
            P("gy", None, None),
            P("gy", None, None),
            P("gy", None),
            P("gy", None, None),
        ),
        out_specs=(P("gx", "gy", None, None), P("gx", "gy", None, None)),
        check_vma=False,
    )
```

```python
import functools

import jax
import jax.numpy as jnp
from jax import lax
from jax.experimental import pallas as pl
from jax.experimental.pallas import tpu as pltpu
from jax.sharding import PartitionSpec as P

F32 = jnp.float32
BF16 = jnp.bfloat16


def moved_to(array, target):
    count_x, count_y = lax.axis_size("gx"), lax.axis_size("gy")
    pairs = []
    for x in range(count_x):
        for y in range(count_y):
            to_x, to_y = target(x, y)
            if 0 <= to_x < count_x and 0 <= to_y < count_y:
                pairs.append((x * count_y + y, to_x * count_y + to_y))
    return lax.ppermute(array, ("gx", "gy"), pairs)


def straight(array, by):
    return moved_to(array, lambda x, y: (x, y + by))


def in_pair(array):
    return moved_to(array, lambda x, y: (x, y ^ 1))


def between_pairs(array):
    return moved_to(array, lambda x, y: (x ^ 2, ((y + 1) ^ 1) - 1))


def quarter(flip, device):
    return jnp.where(flip == 1, device ^ 2, device)


def halves(x):
    high = x.astype(BF16)
    low = (x - high.astype(F32)).astype(BF16)
    return high, low


def product(vector, matrix):
    vector_high, vector_low = halves(vector)
    matrix_high, matrix_low = halves(matrix)
    left = jnp.concatenate([vector_high, vector_low], axis=1)
    right = jnp.concatenate(
        [
            jnp.concatenate([matrix_high, matrix_high], axis=1),
            jnp.concatenate([matrix_low, matrix_low], axis=1),
        ],
        axis=0,
    )
    both = lax.dot_general(left, right, (((1,), (1,)), ((), ())), preferred_element_type=F32)
    width = matrix.shape[0]
    return both[:, :width] + both[:, width:]


def call(kernel, grid, in_specs, out_specs, out_shape, scalars=0, scratch=(), flops=0, moved=0, aliases=None, limit=48):
    return pl.pallas_call(
        kernel,
        grid_spec=pltpu.PrefetchScalarGridSpec(
            num_scalar_prefetch=scalars,
            grid=(grid,),
            in_specs=in_specs,
            out_specs=out_specs,
            scratch_shapes=list(scratch),
        ),
        out_shape=out_shape,
        input_output_aliases=aliases or {},
        compiler_params=pltpu.CompilerParams(vmem_limit_bytes=limit * 1024 * 1024),
        cost_estimate=pl.CostEstimate(flops=40 * flops, bytes_accessed=40 * moved, transcendentals=0),
    )


def part_block(shape, count):
    return pl.BlockSpec((count,) + tuple(shape[1:]), lambda s, *_: (s,) + (0,) * (len(shape) - 1))


def whole(shape):
    return pl.BlockSpec(tuple(shape), lambda s, *_: (0,) * len(shape))


def like(shape):
    return jax.ShapeDtypeStruct(tuple(shape), F32)


def started(ref, buffer, sems, chunks):
    count = buffer.shape[0] // chunks
    copies = []
    for k in range(chunks):
        part = pl.ds(k * count, count)
        copies.append(pltpu.make_async_copy(ref.at[part], buffer.at[part], sems.at[k]))
        copies[-1].start()
    return copies


def restrict_kernel(pos, owner, agg, r_ref, w_ref, pair_ref, own_ref, next_ref, acc, buffer, sems):
    blocks_x, blocks_y = buffer.shape[:2]
    copies = started(r_ref, buffer, sems, blocks_x)
    acc[...] = jnp.zeros_like(acc)
    for p in range(blocks_x):
        copies[p].wait()
        for b in range(blocks_y):
            side = owner[p, b] - pos[1] + 1
            slot = agg[p, b] - pos[0] + 1
            acc[side, slot] += w_ref[p, b][None, :] * buffer[p, b]
    parts, _, rows, _ = own_ref.shape
    for side, flip, ref in (
        (pos[4], pos[3], pair_ref),
        (1, pos[3], own_ref),
        (2 - pos[4], 1 - pos[3], next_ref),
    ):
        for part in range(parts):
            at = pl.multiple_of(quarter(flip, part) * rows, rows)
            ref[part] = acc[side, :, pl.ds(at, rows)]


def put_faces(s, last, core, row_ref, inner, outer, y_first, y_last):
    per, blocks_y = row_ref.shape[:2]
    for t in range(per):
        y_first[t] = row_ref[t, 0]
        y_last[t] = row_ref[t, blocks_y - 1]

    for end, row, lower in ((0, 0, 1), (last, per - 1, 0)):

        @pl.when((s == end) & (core == lower))
        def _():
            inner[...] = row_ref[row]

        @pl.when((s == end) & (core == 1 - lower))
        def _():
            outer[...] = row_ref[row]


def sweep_kernel(pos, r_ref, s_ref, f_ref, inner, outer, y_first, y_last):
    s = pl.program_id(0)
    per, blocks_y = r_ref.shape[:2]
    for t in range(per):
        for b in range(blocks_y):
            f_ref[t, b] = product(r_ref[t, b], s_ref[t, b])
    put_faces(s, pl.num_programs(0) - 1, pos[2], f_ref, inner, outer, y_first, y_last)


def neighbours_off(result, face, before, after, left, right):
    result = result - face[0][None, :] * before
    result = result - face[1][None, :] * after
    result = result - face[2][None, :] * left
    return result - face[3][None, :] * right


def fine_kernel(
    pos,
    r_ref,
    s_ref,
    diag_ref,
    face_ref,
    v_ref,
    x_inner,
    x_outer,
    y_low,
    y_high,
    out_ref,
    before,
    after,
):
    s = pl.program_id(0)
    last = pl.num_programs(0) - 1
    per, blocks_y = r_ref.shape[:2]

    @pl.when((s == 0) & (pos[2] == 0))
    def _():
        before[...] = x_outer[...]

    @pl.when((s == 0) & (pos[2] == 1))
    def _():
        before[...] = x_inner[...]

    @pl.when(s > 0)
    def _():
        before[...] = v_ref[jnp.maximum(s * per - 1, 0)]

    @pl.when((s == last) & (pos[2] == 0))
    def _():
        after[...] = x_inner[...]

    @pl.when((s == last) & (pos[2] == 1))
    def _():
        after[...] = x_outer[...]

    @pl.when(s < last)
    def _():
        after[...] = v_ref[jnp.minimum((s + 1) * per, v_ref.shape[0] - 1)]

    for t in range(per):
        p = s * per + t
        for b in range(blocks_y):
            here = v_ref[p, b]
            image = neighbours_off(
                product(here, diag_ref[t, b]),
                face_ref[t, b],
                before[b] if t == 0 else v_ref[p - 1, b],
                after[b] if t == per - 1 else v_ref[p + 1, b],
                y_low[t] if b == 0 else v_ref[p, b - 1],
                y_high[t] if b == blocks_y - 1 else v_ref[p, b + 1],
            )
            out_ref[t, b] = here + product(r_ref[t, b] - image, s_ref[t, b])


def coarse_first_kernel(got_ref, smooth_ref, rhs_ref, first_ref, sums, buffer, sems):
    parts = sums.shape[0]
    share = sums.shape[1] - 2
    copies = started(smooth_ref, buffer, sems, parts)
    for part in range(parts):
        sums[part] = got_ref[part, 0] + got_ref[part ^ 2, 1]
    for part in range(parts):
        copies[part].wait()
        for i in range(share):
            value = sums[part, i + 1]
            if i == 0 and part > 0:
                value = value + sums[part - 1, share + 1]
            if i == share - 1 and part < parts - 1:
                value = value + sums[part + 1, 0]
            a = part * share + i
            rhs_ref[a] = value
            first_ref[a] = product(value, buffer[a])


def coarse_own_kernel(rhs_ref, first_ref, diag_ref, out_ref, buffer, sems):
    parts = sems.shape[0]
    share = buffer.shape[0] // parts
    copies = started(diag_ref, buffer, sems, parts)
    for part in range(parts):
        copies[part].wait()
        for a in range(part * share, (part + 1) * share):
            out_ref[a] = rhs_ref[a] - product(first_ref[a], buffer[a])


def coarse_last_kernel(
    pos,
    nbr,
    inner_ref,
    pair_ref,
    first_ref,
    next_ref,
    smooth_ref,
    weight_ref,
    out_ref,
    window,
    buffer,
    sems,
    window_sems,
):
    parts, _, slots = out_ref.shape[:3]
    share = slots - 2
    total = window.shape[0] // 3
    copies = started(smooth_ref, buffer, sems, parts)
    moves = []
    for k, (side, ref) in enumerate(((pos[4], pair_ref), (1, first_ref), (2 - pos[4], next_ref))):
        target = window.at[pl.ds(pl.multiple_of(side * total, total), total)]
        moves.append(pltpu.make_async_copy(ref, target, window_sems.at[k]))
        moves[-1].start()
    out_ref[0, 0, 0] = jnp.zeros_like(inner_ref[0])
    out_ref[parts - 1, 0, share + 1] = jnp.zeros_like(inner_ref[0])
    for move in moves:
        move.wait()
    for part in range(parts):
        copies[part].wait()
        for i in range(share):
            a = part * share + i
            value = inner_ref[a]
            for n in range(weight_ref.shape[1]):
                at = nbr[a, n] - (pos[1] - 1) * total
                value = value + weight_ref[a, n][None, :] * window[at]
            value = first_ref[a] + product(value, buffer[a])
            out_ref[part, 0, i + 1] = value
            if i == 0 and part > 0:
                out_ref[part - 1, 0, share + 1] = value
            if i == share - 1 and part < parts - 1:
                out_ref[part + 1, 0, 0] = value
    for part in range(parts):
        out_ref[part ^ 2, 1] = out_ref[part, 0]


def fill_table(pos, pair_ref, own_ref, next_ref, table):
    parts, _, rows, _ = own_ref.shape
    for side, flip, ref in (
        (pos[4], pos[3], pair_ref),
        (1, pos[3], own_ref),
        (2 - pos[4], 1 - pos[3], next_ref),
    ):
        for part in range(parts):
            at = pl.multiple_of(quarter(flip, part) * rows, rows)
            table[side, :, pl.ds(at, rows)] = ref[part]


def corrected(pos, owner, agg, table, fine, weight, p, b):
    side = owner[p, b] - pos[1] + 1
    slot = agg[p, b] - pos[0] + 1
    return fine + weight[None, :] * table[side, slot]


def rim_kernel(
    pos,
    owner,
    agg,
    fine_ref,
    w_ref,
    pair_ref,
    own_ref,
    next_ref,
    inner,
    outer,
    y_first,
    y_last,
    table,
    row_buf,
    col_buf,
    sems,
):
    blocks_x, blocks_y = w_ref.shape[:2]
    ends, sides = (0, blocks_x - 1), (0, blocks_y - 1)
    loads = [(fine_ref.at[:, q], col_buf.at[k]) for k, q in enumerate(sides)]
    loads += [(fine_ref.at[p], row_buf.at[k]) for k, p in enumerate(ends)]
    copies = [pltpu.make_async_copy(a, b, sems.at[k]) for k, (a, b) in enumerate(loads)]
    for copy in copies:
        copy.start()
    fill_table(pos, pair_ref, own_ref, next_ref, table)
    for k, (q, ref) in enumerate(zip(sides, (y_first, y_last))):
        copies[k].wait()
        for p in range(blocks_x):
            ref[p] = corrected(pos, owner, agg, table, col_buf[k, p], w_ref[p, q], p, q)
    for k, p in enumerate(ends):
        copies[2 + k].wait()

        def put(ref):
            for b in range(blocks_y):
                ref[b] = corrected(pos, owner, agg, table, row_buf[k, b], w_ref[p, b], p, b)

        @pl.when(pos[2] == 1 - k)
        def _():
            put(inner)

        @pl.when(pos[2] == k)
        def _():
            put(outer)


def finish_kernel(
    pos,
    owner,
    agg,
    fine_ref,
    w_ref,
    r_ref,
    diag_ref,
    face_ref,
    pair_ref,
    own_ref,
    next_ref,
    out_ref,
    res_ref,
    table,
    solved,
):
    s = pl.program_id(0)
    last = pl.num_programs(0) - 1
    per, blocks_y = fine_ref.shape[:2]
    blocks_x = solved.shape[0] - 2

    @pl.when(s == 0)
    def _():
        fill_table(pos, pair_ref, own_ref, next_ref, table)
        solved[0] = jnp.zeros_like(solved[0])
        solved[blocks_x + 1] = jnp.zeros_like(solved[0])

    @pl.when(s < last)
    def _():
        for t in range(per):
            p = s * per + t
            for b in range(blocks_y):
                value = corrected(pos, owner, agg, table, fine_ref[t, b], w_ref[t, b], p, b)
                solved[p + 1, b] = value
                out_ref[t, b] = value

    @pl.when(s > 0)
    def _():
        for t in range(per):
            p = (s - 1) * per + t
            for b in range(blocks_y):
                face = face_ref[t, b]
                value = r_ref[t, b] - product(solved[p + 1, b], diag_ref[t, b])
                value = value + face[0][None, :] * solved[p, b]
                value = value + face[1][None, :] * solved[p + 2, b]
                if b > 0:
                    value = value + face[2][None, :] * solved[p + 1, b - 1]
                if b < blocks_y - 1:
                    value = value + face[3][None, :] * solved[p + 1, b + 1]
                res_ref[t, b] = value


def border_kernel(
    pos, part_ref, face_ref, x_inner, x_outer, y_low, y_high, out_ref, row_buf, col_buf, sems
):
    blocks_x, blocks_y = face_ref.shape[:2]
    core = pos[2]
    ends = (0, blocks_x - 1)
    sides = (0, blocks_y - 1)
    inside = pl.ds(1, blocks_x - 2)
    pairs = [(out_ref.at[p], row_buf.at[k]) for k, p in enumerate(ends)]
    pairs += [(out_ref.at[inside, q], col_buf.at[k]) for k, q in enumerate(sides)]
    loads = [pltpu.make_async_copy(a, b, sems.at[k]) for k, (a, b) in enumerate(pairs)]
    for load in loads:
        load.start()
    for load in loads:
        load.wait()
    for k, p in enumerate(ends):
        lower = core == k
        for b in range(blocks_y):
            beyond = jnp.where(lower, x_outer[b], x_inner[b])
            row_buf[k, b] += face_ref[p, b, k][None, :] * beyond
    for k, (q, halo_ref) in enumerate(zip(sides, (y_low, y_high))):
        for j, p in enumerate(ends):
            row_buf[j, q] += face_ref[p, q, 2 + k][None, :] * halo_ref[p]
        for p in range(1, blocks_x - 1):
            col_buf[k, p - 1] += face_ref[p, q, 2 + k][None, :] * halo_ref[p]
    stores = [pltpu.make_async_copy(b, a, sems.at[4 + k]) for k, (a, b) in enumerate(pairs)]
    for store in stores:
        store.start()
    for store in stores:
        store.wait()


def to_sibling(array):
    return moved_to(array, lambda x, y: (x ^ 1, y))


def halo(faces):
    inner, outer, y_first, y_last = faces
    y_low = straight(y_last, 1)
    y_high = straight(y_first, -1)
    x_inner = to_sibling(inner)
    x_outer = moved_to(outer, lambda x, y: (((x + 1) ^ 1) - 1, y))
    return x_inner, x_outer, y_low, y_high


def body(
    right_side,
    diag_blocks,
    smoother,
    face_weight,
    restrict_weight,
    prolong_weight,
    block_owner,
    block_aggregate,
    coarse_diag,
    coarse_smooth,
    neighbors,
    neighbor_weight,
):
    blocks_x, blocks_y, rows, size = right_side.shape
    total = coarse_diag.shape[0]
    parts = lax.axis_size("gx")
    share = total // parts
    per = 2
    steps = blocks_x // per
    fine_shape = right_side.shape
    mat_shape = diag_blocks.shape
    slab = (parts, share + 2, rows // parts, size)
    double = (parts, 2) + slab[1:]
    coarse_shape = (total, rows // parts, size)
    x_face = (blocks_y, rows, size)
    y_face = (blocks_x, rows, size)
    block_flops = 2 * 4 * rows * size * size
    fine_count = blocks_x * blocks_y
    fine_bytes = fine_count * rows * size * 4
    coarse_flops = total * block_flops // parts
    coarse_bytes = total * size * size * 4
    hbm = pl.BlockSpec(memory_space=pl.ANY)
    fine_block = part_block(fine_shape, per)
    mat_block = part_block(mat_shape, per)
    weight_block = part_block(face_weight.shape, per)
    vmem = pl.BlockSpec(memory_space=pltpu.VMEM)
    cmat_scratch = [
        pltpu.VMEM(coarse_diag.shape, F32),
        pltpu.SemaphoreType.DMA((parts,)),
    ]
    face_specs = [whole(x_face)] * 2 + [part_block(y_face, per)] * 2
    face_shapes = [like(x_face)] * 2 + [like(y_face)] * 2

    gx, gy = lax.axis_index("gx"), lax.axis_index("gy")
    pos = jnp.stack([gx * share, gy, gx % 2, gy // 2 % 2, 2 * (1 - gy % 2)]).astype(jnp.int32)

    to_pair, own, to_next = call(
        restrict_kernel,
        1,
        [hbm, whole(restrict_weight.shape)],
        [vmem] * 3,
        [like(slab)] * 3,
        scalars=3,
        scratch=[
            pltpu.VMEM((3, share + 2, rows, size), F32),
            pltpu.VMEM(fine_shape, F32),
            pltpu.SemaphoreType.DMA((blocks_x,)),
        ],
        moved=2 * fine_bytes,
    )(pos, block_owner, block_aggregate, right_side, restrict_weight)

    from_pair = in_pair(to_pair)
    from_next = between_pairs(to_next)

    sweep, *faces = call(
        sweep_kernel,
        steps,
        [fine_block, mat_block],
        [fine_block] + face_specs,
        [like(fine_shape)] + face_shapes,
        scalars=1,
        flops=fine_count * block_flops,
        moved=3 * fine_bytes,
    )(pos, right_side, smoother)

    own, from_pair, from_next, sweep = lax.optimization_barrier(
        (own, from_pair, from_next, sweep)
    )
    got = lax.all_to_all(
        jnp.stack([own + from_pair, from_next], axis=1), "gx", 0, 0, tiled=True
    )

    rhs, first = call(
        coarse_first_kernel,
        1,
        [vmem, hbm],
        [vmem] * 2,
        [like(coarse_shape)] * 2,
        scratch=[pltpu.VMEM(slab, F32)] + cmat_scratch,
        flops=coarse_flops,
        moved=coarse_bytes,
    )(got, coarse_smooth)

    first, rhs, faces = lax.optimization_barrier((first, rhs, faces))
    sweep_halo = halo(faces)
    pair_first = in_pair(first)
    next_first = between_pairs(first)

    inner = call(
        coarse_own_kernel,
        1,
        [vmem, vmem, hbm],
        vmem,
        like(coarse_shape),
        scratch=cmat_scratch,
        flops=coarse_flops,
        moved=coarse_bytes,
    )(rhs, first, coarse_diag)

    corr = call(
        coarse_last_kernel,
        1,
        [vmem] * 4 + [hbm, vmem],
        vmem,
        like(double),
        scalars=2,
        scratch=[pltpu.VMEM((3 * total,) + coarse_shape[1:], F32)]
        + cmat_scratch
        + [pltpu.SemaphoreType.DMA((3,))],
        flops=coarse_flops,
        moved=coarse_bytes,
    )(pos, neighbors, inner, pair_first, first, next_first, coarse_smooth, neighbor_weight)

    x_inner, x_outer, y_low, y_high = sweep_halo
    corr, x_outer, y_low = lax.optimization_barrier((corr, x_outer, y_low))
    sweep_halo = (x_inner, x_outer, y_low, y_high)
    mine = lax.all_to_all(corr, "gx", 0, 0, tiled=True)
    tables = (in_pair(mine[:, 0]), mine[:, 0], between_pairs(mine[:, 1]))

    fine_part = call(
        fine_kernel,
        steps,
        [fine_block] + [mat_block] * 2 + [weight_block, whole(fine_shape)]
        + [vmem] * 2
        + [part_block(y_face, per)] * 2,
        fine_block,
        like(fine_shape),
        scalars=1,
        scratch=[pltpu.VMEM(x_face, F32)] * 2,
        flops=2 * fine_count * block_flops,
        moved=5 * fine_bytes,
    )(pos, right_side, smoother, diag_blocks, face_weight, sweep, *sweep_halo)

    rim = call(
        rim_kernel,
        1,
        [hbm] + [vmem] * 4,
        [vmem] * 4,
        face_shapes,
        scalars=3,
        scratch=[
            pltpu.VMEM((3, share + 2, rows, size), F32),
            pltpu.VMEM((2,) + x_face, F32),
            pltpu.VMEM((2,) + y_face, F32),
            pltpu.SemaphoreType.DMA((4,)),
        ],
        moved=fine_bytes,
    )(pos, block_owner, block_aggregate, fine_part, prolong_weight, *tables)
    solved_halo = halo(rim)

    def now(shape):
        return pl.BlockSpec(
            (per,) + tuple(shape[1:]),
            lambda s, *_: (jnp.minimum(s, steps - 1),) + (0,) * (len(shape) - 1),
        )

    def previous(shape):
        return pl.BlockSpec(
            (per,) + tuple(shape[1:]),
            lambda s, *_: (jnp.maximum(s - 1, 0),) + (0,) * (len(shape) - 1),
        )

    solved, residual = call(
        finish_kernel,
        steps + 1,
        [
            now(fine_shape),
            now(prolong_weight.shape),
            previous(fine_shape),
            previous(mat_shape),
            previous(face_weight.shape),
        ]
        + [vmem] * 3,
        [now(fine_shape), previous(fine_shape)],
        [like(fine_shape)] * 2,
        scalars=3,
        scratch=[
            pltpu.VMEM((3, share + 2, rows, size), F32),
            pltpu.VMEM((blocks_x + 2, blocks_y, rows, size), F32),
        ],
        flops=fine_count * block_flops,
        moved=5 * fine_bytes,
    )(
        pos,
        block_owner,
        block_aggregate,
        fine_part,
        prolong_weight,
        right_side,
        diag_blocks,
        face_weight,
        *tables,
    )

    residual = call(
        border_kernel,
        1,
        [hbm, whole(face_weight.shape)] + [vmem] * 4,
        hbm,
        like(fine_shape),
        scalars=1,
        scratch=[
            pltpu.VMEM((2,) + x_face, F32),
            pltpu.VMEM((2, blocks_x - 2, rows, size), F32),
            pltpu.SemaphoreType.DMA((8,)),
        ],
        moved=fine_bytes,
        aliases={1: 0},
    )(pos, residual, face_weight, *solved_halo)
    return (solved, residual)


def solution(mesh):
    return jax.shard_map(
        body,
        mesh=mesh,
        in_specs=(
            P("gx", "gy", None, None),
            P("gx", "gy", None, None),
            P("gx", "gy", None, None),
            P("gx", "gy", None, None),
            P("gx", "gy", None),
            P("gx", "gy", None),
            P("gx", "gy"),
            P("gx", "gy"),
            P("gy", None, None),
            P("gy", None, None),
            P("gy", None),
            P("gy", None, None),
        ),
        out_specs=(P("gx", "gy", None, None), P("gx", "gy", None, None)),
        check_vma=False,
    )
```

```python
import functools

import jax
import jax.numpy as jnp
from jax import lax
from jax.experimental import pallas as pl
from jax.experimental.pallas import tpu as pltpu
from jax.sharding import PartitionSpec as P

F32 = jnp.float32
BF16 = jnp.bfloat16


def moved_to(array, target):
    count_x, count_y = lax.axis_size("gx"), lax.axis_size("gy")
    pairs = []
    for x in range(count_x):
        for y in range(count_y):
            to_x, to_y = target(x, y)
            if 0 <= to_x < count_x and 0 <= to_y < count_y:
                pairs.append((x * count_y + y, to_x * count_y + to_y))
    return lax.ppermute(array, ("gx", "gy"), pairs)


def in_pair(array):
    return moved_to(array, lambda x, y: (x, y ^ 1))


def between_pairs(array):
    return moved_to(array, lambda x, y: (x ^ 2, ((y + 1) ^ 1) - 1))


def in_pair_crossed(array):
    return moved_to(array, lambda x, y: (x ^ 2, y ^ 1))


def quarter(flip, device):
    return jnp.where(flip == 1, device ^ 2, device)


def halves(x):
    high = x.astype(BF16)
    low = (x - high.astype(F32)).astype(BF16)
    return high, low


def product(vector, matrix):
    vector_high, vector_low = halves(vector)
    matrix_high, matrix_low = halves(matrix)
    left = jnp.concatenate([vector_high, vector_low], axis=1)
    right = jnp.concatenate(
        [
            jnp.concatenate([matrix_high, matrix_high], axis=1),
            jnp.concatenate([matrix_low, matrix_low], axis=1),
        ],
        axis=0,
    )
    both = lax.dot_general(left, right, (((1,), (1,)), ((), ())), preferred_element_type=F32)
    width = matrix.shape[0]
    return both[:, :width] + both[:, width:]


def call(kernel, grid, in_specs, out_specs, out_shape, scalars=0, scratch=(), flops=0, moved=0, aliases=None, limit=32):
    return pl.pallas_call(
        kernel,
        grid_spec=pltpu.PrefetchScalarGridSpec(
            num_scalar_prefetch=scalars,
            grid=(grid,),
            in_specs=in_specs,
            out_specs=out_specs,
            scratch_shapes=list(scratch),
        ),
        out_shape=out_shape,
        input_output_aliases=aliases or {},
        compiler_params=pltpu.CompilerParams(vmem_limit_bytes=limit * 1024 * 1024),
        cost_estimate=pl.CostEstimate(flops=40 * flops, bytes_accessed=40 * moved, transcendentals=0),
    )


def part_block(shape, count):
    return pl.BlockSpec((count,) + tuple(shape[1:]), lambda s, *_: (s,) + (0,) * (len(shape) - 1))


def whole(shape):
    return pl.BlockSpec(tuple(shape), lambda s, *_: (0,) * len(shape))


def like(shape):
    return jax.ShapeDtypeStruct(tuple(shape), F32)


def started(ref, buffer, sems, chunks):
    count = buffer.shape[0] // chunks
    copies = []
    for k in range(chunks):
        part = pl.ds(k * count, count)
        copies.append(pltpu.make_async_copy(ref.at[part], buffer.at[part], sems.at[k]))
        copies[-1].start()
    return copies


def restrict_kernel(pos, owner, agg, r_ref, w_ref, pair_ref, own_ref, next_ref, acc, buffer, sems):
    blocks_x, blocks_y = buffer.shape[:2]
    copies = started(r_ref, buffer, sems, blocks_x)
    acc[...] = jnp.zeros_like(acc)
    for p in range(blocks_x):
        copies[p].wait()
        for b in range(blocks_y):
            side = owner[p, b] - pos[1] + 1
            slot = agg[p, b] - pos[0] + 1
            acc[side, slot] += w_ref[p, b][None, :] * buffer[p, b]
    parts, _, rows, _ = own_ref.shape
    for side, flip, ref in (
        (pos[4], 1 - pos[3], pair_ref),
        (1, pos[3], own_ref),
        (2 - pos[4], 1 - pos[3], next_ref),
    ):
        for part in range(parts):
            at = pl.multiple_of(quarter(flip, part) * rows, rows)
            ref[part] = acc[side, :, pl.ds(at, rows)]


def put_faces(s, last, pos, row_ref, inner, outer, y_pair, y_next):
    per, blocks_y = row_ref.shape[:2]
    core = pos[2]
    pair_side = jnp.where(pos[4] == 2, blocks_y - 1, 0)
    for t in range(per):
        y_pair[t] = row_ref[t, pair_side]
        y_next[t] = row_ref[t, blocks_y - 1 - pair_side]

    for end, row, lower in ((0, 0, 1), (last, per - 1, 0)):

        @pl.when((s == end) & (core == lower))
        def _():
            inner[...] = row_ref[row]

        @pl.when((s == end) & (core == 1 - lower))
        def _():
            outer[...] = row_ref[row]


def sweep_kernel(pos, r_ref, s_ref, f_ref, inner, outer, y_pair, y_next):
    s = pl.program_id(0)
    per, blocks_y = r_ref.shape[:2]
    for t in range(per):
        for b in range(blocks_y):
            f_ref[t, b] = product(r_ref[t, b], s_ref[t, b])
    put_faces(s, pl.num_programs(0) - 1, pos, f_ref, inner, outer, y_pair, y_next)


def neighbours_off(result, face, before, after, left, right):
    result = result - face[0][None, :] * before
    result = result - face[1][None, :] * after
    result = result - face[2][None, :] * left
    return result - face[3][None, :] * right


def fine_kernel(
    pos,
    r_ref,
    s_ref,
    diag_ref,
    face_ref,
    v_ref,
    x_inner,
    x_outer,
    y_pair,
    y_next,
    out_ref,
    before,
    after,
):
    s = pl.program_id(0)
    last = pl.num_programs(0) - 1
    per, blocks_y = r_ref.shape[:2]

    @pl.when((s == 0) & (pos[2] == 0))
    def _():
        before[...] = x_outer[...]

    @pl.when((s == 0) & (pos[2] == 1))
    def _():
        before[...] = x_inner[...]

    @pl.when(s > 0)
    def _():
        before[...] = v_ref[jnp.maximum(s * per - 1, 0)]

    @pl.when((s == last) & (pos[2] == 0))
    def _():
        after[...] = x_inner[...]

    @pl.when((s == last) & (pos[2] == 1))
    def _():
        after[...] = x_outer[...]

    @pl.when(s < last)
    def _():
        after[...] = v_ref[jnp.minimum((s + 1) * per, v_ref.shape[0] - 1)]

    even = pos[4] == 2

    def low_side(t):
        return jnp.where(even, y_next[t], y_pair[t])

    def high_side(t):
        return jnp.where(even, y_pair[t], y_next[t])

    for t in range(per):
        p = s * per + t
        for b in range(blocks_y):
            here = v_ref[p, b]
            image = neighbours_off(
                product(here, diag_ref[t, b]),
                face_ref[t, b],
                before[b] if t == 0 else v_ref[p - 1, b],
                after[b] if t == per - 1 else v_ref[p + 1, b],
                low_side(t) if b == 0 else v_ref[p, b - 1],
                high_side(t) if b == blocks_y - 1 else v_ref[p, b + 1],
            )
            out_ref[t, b] = here + product(r_ref[t, b] - image, s_ref[t, b])


def coarse_first_kernel(got_ref, smooth_ref, rhs_ref, first_ref, sums, buffer, sems):
    parts = sums.shape[0]
    share = sums.shape[1] - 2
    copies = started(smooth_ref, buffer, sems, parts)
    for part in range(parts):
        sums[part] = got_ref[part, 0] + got_ref[part ^ 2, 1]
    for part in range(parts):
        copies[part].wait()
        for i in range(share):
            value = sums[part, i + 1]
            if i == 0 and part > 0:
                value = value + sums[part - 1, share + 1]
            if i == share - 1 and part < parts - 1:
                value = value + sums[part + 1, 0]
            a = part * share + i
            rhs_ref[a] = value
            first_ref[a] = product(value, buffer[a])


def coarse_own_kernel(rhs_ref, first_ref, diag_ref, out_ref, buffer, sems):
    parts = sems.shape[0]
    share = buffer.shape[0] // parts
    copies = started(diag_ref, buffer, sems, parts)
    for part in range(parts):
        copies[part].wait()
        for a in range(part * share, (part + 1) * share):
            out_ref[a] = rhs_ref[a] - product(first_ref[a], buffer[a])


def coarse_last_kernel(
    pos,
    nbr,
    inner_ref,
    pair_ref,
    first_ref,
    next_ref,
    smooth_ref,
    weight_ref,
    out_ref,
    window,
    buffer,
    sems,
    window_sems,
):
    parts, _, slots = out_ref.shape[:3]
    share = slots - 2
    total = window.shape[0] // 3
    copies = started(smooth_ref, buffer, sems, parts)
    moves = []
    for k, (side, ref) in enumerate(((pos[4], pair_ref), (1, first_ref), (2 - pos[4], next_ref))):
        target = window.at[pl.ds(pl.multiple_of(side * total, total), total)]
        moves.append(pltpu.make_async_copy(ref, target, window_sems.at[k]))
        moves[-1].start()
    out_ref[0, 0, 0] = jnp.zeros_like(inner_ref[0])
    out_ref[parts - 1, 0, share + 1] = jnp.zeros_like(inner_ref[0])
    for move in moves:
        move.wait()
    for part in range(parts):
        copies[part].wait()
        for i in range(share):
            a = part * share + i
            value = inner_ref[a]
            for n in range(weight_ref.shape[1]):
                at = nbr[a, n] - (pos[1] - 1) * total
                value = value + weight_ref[a, n][None, :] * window[at]
            value = first_ref[a] + product(value, buffer[a])
            out_ref[part, 0, i + 1] = value
            if i == 0 and part > 0:
                out_ref[part - 1, 0, share + 1] = value
            if i == share - 1 and part < parts - 1:
                out_ref[part + 1, 0, 0] = value
    for part in range(parts):
        out_ref[part ^ 2, 1] = out_ref[part, 0]


def fill_table(pos, pair_ref, own_ref, next_ref, table):
    parts, _, rows, _ = own_ref.shape
    for side, flip, ref in (
        (pos[4], 1 - pos[3], pair_ref),
        (1, pos[3], own_ref),
        (2 - pos[4], 1 - pos[3], next_ref),
    ):
        for part in range(parts):
            at = pl.multiple_of(quarter(flip, part) * rows, rows)
            table[side, :, pl.ds(at, rows)] = ref[part]


def corrected(pos, owner, agg, table, fine, weight, p, b):
    side = owner[p, b] - pos[1] + 1
    slot = agg[p, b] - pos[0] + 1
    return fine + weight[None, :] * table[side, slot]


def rim_kernel(
    pos, owner, agg, fine_ref, w_ref, pair_ref, own_ref, next_ref, y_pair, y_next, table, col_buf, sems
):
    blocks_x, blocks_y = w_ref.shape[:2]
    copies = []
    for k in range(2):
        source = fine_ref.at[:, k * (blocks_y - 1)]
        copies.append(pltpu.make_async_copy(source, col_buf.at[k], sems.at[k]))
        copies[-1].start()
    fill_table(pos, pair_ref, own_ref, next_ref, table)
    for copy in copies:
        copy.wait()
    pair_at = jnp.where(pos[4] == 2, 1, 0)
    for at, ref in ((1 - pair_at, y_next), (pair_at, y_pair)):
        q = at * (blocks_y - 1)
        for p in range(blocks_x):
            ref[p] = corrected(pos, owner, agg, table, col_buf[at, p], w_ref[p, q], p, q)


def finish_kernel(
    pos,
    owner,
    agg,
    fine_ref,
    w_ref,
    r_ref,
    diag_ref,
    face_ref,
    pair_ref,
    own_ref,
    next_ref,
    out_ref,
    res_ref,
    inner,
    outer,
    table,
    solved,
):
    s = pl.program_id(0)
    last = pl.num_programs(0) - 1
    per, blocks_y = fine_ref.shape[:2]
    blocks_x = solved.shape[0] - 2

    @pl.when(s == 0)
    def _():
        fill_table(pos, pair_ref, own_ref, next_ref, table)
        solved[0] = jnp.zeros_like(solved[0])
        solved[blocks_x + 1] = jnp.zeros_like(solved[0])

    @pl.when(s < last)
    def _():
        for t in range(per):
            p = s * per + t
            for b in range(blocks_y):
                value = corrected(pos, owner, agg, table, fine_ref[t, b], w_ref[t, b], p, b)
                solved[p + 1, b] = value
                out_ref[t, b] = value
        for end, row, lower in ((0, 0, 1), (last - 1, per - 1, 0)):

            @pl.when((s == end) & (pos[2] == lower))
            def _():
                inner[...] = out_ref[row]

            @pl.when((s == end) & (pos[2] == 1 - lower))
            def _():
                outer[...] = out_ref[row]

    @pl.when(s > 0)
    def _():
        for t in range(per):
            p = (s - 1) * per + t
            for b in range(blocks_y):
                face = face_ref[t, b]
                value = r_ref[t, b] - product(solved[p + 1, b], diag_ref[t, b])
                value = value + face[0][None, :] * solved[p, b]
                value = value + face[1][None, :] * solved[p + 2, b]
                if b > 0:
                    value = value + face[2][None, :] * solved[p + 1, b - 1]
                if b < blocks_y - 1:
                    value = value + face[3][None, :] * solved[p + 1, b + 1]
                res_ref[t, b] = value


def border_kernel(
    pos, part_ref, face_ref, x_inner, x_outer, y_pair, y_next, out_ref, row_buf, col_buf, sems
):
    blocks_x, blocks_y = face_ref.shape[:2]
    core = pos[2]
    ends = (0, blocks_x - 1)
    sides = (0, blocks_y - 1)
    inside = pl.ds(1, blocks_x - 2)
    pairs = [(out_ref.at[p], row_buf.at[k]) for k, p in enumerate(ends)]
    pairs += [(out_ref.at[inside, q], col_buf.at[k]) for k, q in enumerate(sides)]
    loads = [pltpu.make_async_copy(a, b, sems.at[k]) for k, (a, b) in enumerate(pairs)]
    for load in loads:
        load.start()
    for load in loads:
        load.wait()
    for k, p in enumerate(ends):
        lower = core == k
        for b in range(blocks_y):
            beyond = jnp.where(lower, x_outer[b], x_inner[b])
            row_buf[k, b] += face_ref[p, b, k][None, :] * beyond
    even = pos[4] == 2
    for k, q in enumerate(sides):
        from_pair = even if k == 1 else jnp.logical_not(even)

        def beyond_y(p):
            return jnp.where(from_pair, y_pair[p], y_next[p])

        for j, p in enumerate(ends):
            row_buf[j, q] += face_ref[p, q, 2 + k][None, :] * beyond_y(p)
        for p in range(1, blocks_x - 1):
            col_buf[k, p - 1] += face_ref[p, q, 2 + k][None, :] * beyond_y(p)
    stores = [pltpu.make_async_copy(b, a, sems.at[4 + k]) for k, (a, b) in enumerate(pairs)]
    for store in stores:
        store.start()
    for store in stores:
        store.wait()


def to_sibling(array):
    return moved_to(array, lambda x, y: (x ^ 1, y))


def x_halo(inner, outer):
    return to_sibling(inner), moved_to(outer, lambda x, y: (((x + 1) ^ 1) - 1, y))


def y_halo(y_pair, y_next):
    return in_pair(y_pair), moved_to(y_next, lambda x, y: (x, ((y + 1) ^ 1) - 1))


def body(
    right_side,
    diag_blocks,
    smoother,
    face_weight,
    restrict_weight,
    prolong_weight,
    block_owner,
    block_aggregate,
    coarse_diag,
    coarse_smooth,
    neighbors,
    neighbor_weight,
):
    blocks_x, blocks_y, rows, size = right_side.shape
    total = coarse_diag.shape[0]
    parts = lax.axis_size("gx")
    share = total // parts
    per = 2
    steps = blocks_x // per
    fine_shape = right_side.shape
    mat_shape = diag_blocks.shape
    slab = (parts, share + 2, rows // parts, size)
    double = (parts, 2) + slab[1:]
    coarse_shape = (total, rows // parts, size)
    x_face = (blocks_y, rows, size)
    y_face = (blocks_x, rows, size)
    block_flops = 2 * 4 * rows * size * size
    fine_count = blocks_x * blocks_y
    fine_bytes = fine_count * rows * size * 4
    coarse_flops = total * block_flops // parts
    coarse_bytes = total * size * size * 4
    hbm = pl.BlockSpec(memory_space=pl.ANY)
    fine_block = part_block(fine_shape, per)
    mat_block = part_block(mat_shape, per)
    weight_block = part_block(face_weight.shape, per)
    vmem = pl.BlockSpec(memory_space=pltpu.VMEM)
    cmat_scratch = [
        pltpu.VMEM(coarse_diag.shape, F32),
        pltpu.SemaphoreType.DMA((parts,)),
    ]
    face_specs = [whole(x_face)] * 2 + [part_block(y_face, per)] * 2
    face_shapes = [like(x_face)] * 2 + [like(y_face)] * 2

    gx, gy = lax.axis_index("gx"), lax.axis_index("gy")
    pos = jnp.stack([gx * share, gy, gx % 2, gy % 2, 2 * (1 - gy % 2)]).astype(jnp.int32)

    to_pair, own, to_next = call(
        restrict_kernel,
        1,
        [hbm, whole(restrict_weight.shape)],
        [vmem] * 3,
        [like(slab)] * 3,
        scalars=3,
        scratch=[
            pltpu.VMEM((3, share + 2, rows, size), F32),
            pltpu.VMEM(fine_shape, F32),
            pltpu.SemaphoreType.DMA((blocks_x,)),
        ],
        moved=2 * fine_bytes,
    )(pos, block_owner, block_aggregate, right_side, restrict_weight)

    from_pair = in_pair(to_pair)
    from_next = between_pairs(to_next)

    sweep, *faces = call(
        sweep_kernel,
        steps,
        [fine_block, mat_block],
        [fine_block] + face_specs,
        [like(fine_shape)] + face_shapes,
        scalars=1,
        flops=fine_count * block_flops,
        moved=3 * fine_bytes,
    )(pos, right_side, smoother)

    own, from_pair, from_next, sweep_x = lax.optimization_barrier(
        (own, from_pair, from_next, x_halo(*faces[:2]))
    )
    got = lax.all_to_all(
        jnp.stack([own + from_pair, from_next], axis=1), "gx", 0, 0, tiled=True
    )

    rhs, first = call(
        coarse_first_kernel,
        1,
        [vmem, hbm],
        [vmem] * 2,
        [like(coarse_shape)] * 2,
        scratch=[pltpu.VMEM(slab, F32)] + cmat_scratch,
        flops=coarse_flops,
        moved=coarse_bytes,
    )(got, coarse_smooth)

    first, rhs, y_faces = lax.optimization_barrier((first, rhs, faces[2:]))
    sweep_y = y_halo(*y_faces)
    pair_first = in_pair_crossed(first)
    next_first = between_pairs(first)

    inner = call(
        coarse_own_kernel,
        1,
        [vmem, vmem, hbm],
        vmem,
        like(coarse_shape),
        scratch=cmat_scratch,
        flops=coarse_flops,
        moved=coarse_bytes,
    )(rhs, first, coarse_diag)

    corr = call(
        coarse_last_kernel,
        1,
        [vmem] * 4 + [hbm, vmem],
        vmem,
        like(double),
        scalars=2,
        scratch=[pltpu.VMEM((3 * total,) + coarse_shape[1:], F32)]
        + cmat_scratch
        + [pltpu.SemaphoreType.DMA((3,))],
        flops=coarse_flops,
        moved=coarse_bytes,
    )(pos, neighbors, inner, pair_first, first, next_first, coarse_smooth, neighbor_weight)

    corr, sweep_y = lax.optimization_barrier((corr, sweep_y))
    mine = lax.all_to_all(corr, "gx", 0, 0, tiled=True)
    tables = (in_pair(mine[:, 0]), mine[:, 0], between_pairs(mine[:, 1]))

    fine_part = call(
        fine_kernel,
        steps,
        [fine_block] + [mat_block] * 2 + [weight_block, whole(fine_shape)]
        + [whole(x_face)] * 2
        + [part_block(y_face, per)] * 2,
        fine_block,
        like(fine_shape),
        scalars=1,
        scratch=[pltpu.VMEM(x_face, F32)] * 2,
        flops=2 * fine_count * block_flops,
        moved=5 * fine_bytes,
    )(pos, right_side, smoother, diag_blocks, face_weight, sweep, *sweep_x, *sweep_y)

    rim = call(
        rim_kernel,
        1,
        [hbm, whole(prolong_weight.shape)] + [vmem] * 3,
        [vmem] * 2,
        [like(y_face)] * 2,
        scalars=3,
        scratch=[
            pltpu.VMEM((3, share + 2, rows, size), F32),
            pltpu.VMEM((2,) + y_face, F32),
            pltpu.SemaphoreType.DMA((2,)),
        ],
        moved=fine_bytes,
    )(pos, block_owner, block_aggregate, fine_part, prolong_weight, *tables)
    solved_y = y_halo(*rim)

    def now(shape):
        return pl.BlockSpec(
            (per,) + tuple(shape[1:]),
            lambda s, *_: (jnp.minimum(s, steps - 1),) + (0,) * (len(shape) - 1),
        )

    def previous(shape):
        return pl.BlockSpec(
            (per,) + tuple(shape[1:]),
            lambda s, *_: (jnp.maximum(s - 1, 0),) + (0,) * (len(shape) - 1),
        )

    solved, residual, *x_faces = call(
        finish_kernel,
        steps + 1,
        [
            now(fine_shape),
            now(prolong_weight.shape),
            previous(fine_shape),
            previous(mat_shape),
            previous(face_weight.shape),
        ]
        + [vmem] * 3,
        [now(fine_shape), previous(fine_shape)] + [vmem] * 2,
        [like(fine_shape)] * 2 + [like(x_face)] * 2,
        scalars=3,
        scratch=[
            pltpu.VMEM((3, share + 2, rows, size), F32),
            pltpu.VMEM((blocks_x + 2, blocks_y, rows, size), F32),
        ],
        flops=fine_count * block_flops,
        moved=5 * fine_bytes,
    )(
        pos,
        block_owner,
        block_aggregate,
        fine_part,
        prolong_weight,
        right_side,
        diag_blocks,
        face_weight,
        *tables,
    )

    residual = call(
        border_kernel,
        1,
        [hbm, whole(face_weight.shape)] + [vmem] * 4,
        hbm,
        like(fine_shape),
        scalars=1,
        scratch=[
            pltpu.VMEM((2,) + x_face, F32),
            pltpu.VMEM((2, blocks_x - 2, rows, size), F32),
            pltpu.SemaphoreType.DMA((8,)),
        ],
        moved=fine_bytes,
        aliases={1: 0},
    )(pos, residual, face_weight, *x_halo(*x_faces), *solved_y)
    return (solved, residual)


def solution(mesh):
    return jax.shard_map(
        body,
        mesh=mesh,
        in_specs=(
            P("gx", "gy", None, None),
            P("gx", "gy", None, None),
            P("gx", "gy", None, None),
            P("gx", "gy", None, None),
            P("gx", "gy", None),
            P("gx", "gy", None),
            P("gx", "gy"),
            P("gx", "gy"),
            P("gy", None, None),
            P("gy", None, None),
            P("gy", None),
            P("gy", None, None),
        ),
        out_specs=(P("gx", "gy", None, None), P("gx", "gy", None, None)),
        check_vma=False,
    )
```

```python
import functools

import jax
import jax.numpy as jnp
from jax import lax
from jax.experimental import pallas as pl
from jax.experimental.pallas import tpu as pltpu
from jax.sharding import PartitionSpec as P

F32 = jnp.float32
BF16 = jnp.bfloat16


def moved_to(array, target):
    count_x, count_y = lax.axis_size("gx"), lax.axis_size("gy")
    pairs = []
    for x in range(count_x):
        for y in range(count_y):
            to_x, to_y = target(x, y)
            if 0 <= to_x < count_x and 0 <= to_y < count_y:
                pairs.append((x * count_y + y, to_x * count_y + to_y))
    return lax.ppermute(array, ("gx", "gy"), pairs)


def in_pair(array):
    return moved_to(array, lambda x, y: (x, y ^ 1))


def in_pair_crossed(array):
    return moved_to(array, lambda x, y: (x ^ 2, y ^ 1))


def between_pairs(array):
    return moved_to(array, lambda x, y: (x, ((y + 1) ^ 1) - 1))


def between_pairs_crossed(array):
    return moved_to(array, lambda x, y: (x ^ 2, ((y + 1) ^ 1) - 1))


def to_partner(array):
    return moved_to(array, lambda x, y: (x ^ 2, y))


def quarter(flip, chip, core):
    return 2 * jnp.where(flip == 1, 1 - chip, chip) + core


def halves(x):
    high = x.astype(BF16)
    low = (x - high.astype(F32)).astype(BF16)
    return high, low


def product(vector, matrix):
    vector_high, vector_low = halves(vector)
    matrix_high, matrix_low = halves(matrix)
    left = jnp.concatenate([vector_high, vector_low], axis=1)
    right = jnp.concatenate(
        [
            jnp.concatenate([matrix_high, matrix_high], axis=1),
            jnp.concatenate([matrix_low, matrix_low], axis=1),
        ],
        axis=0,
    )
    both = lax.dot_general(left, right, (((1,), (1,)), ((), ())), preferred_element_type=F32)
    width = matrix.shape[0]
    return both[:, :width] + both[:, width:]


def call(kernel, grid, in_specs, out_specs, out_shape, scalars=0, scratch=(), flops=0, moved=0, aliases=None, limit=32):
    return pl.pallas_call(
        kernel,
        grid_spec=pltpu.PrefetchScalarGridSpec(
            num_scalar_prefetch=scalars,
            grid=(grid,),
            in_specs=in_specs,
            out_specs=out_specs,
            scratch_shapes=list(scratch),
        ),
        out_shape=out_shape,
        input_output_aliases=aliases or {},
        compiler_params=pltpu.CompilerParams(vmem_limit_bytes=limit * 1024 * 1024),
        cost_estimate=pl.CostEstimate(flops=40 * flops, bytes_accessed=40 * moved, transcendentals=0),
    )


def part_block(shape, count):
    return pl.BlockSpec((count,) + tuple(shape[1:]), lambda s, *_: (s,) + (0,) * (len(shape) - 1))


def whole(shape):
    return pl.BlockSpec(tuple(shape), lambda s, *_: (0,) * len(shape))


def like(shape):
    return jax.ShapeDtypeStruct(tuple(shape), F32)


def started(ref, buffer, sems, chunks):
    count = buffer.shape[0] // chunks
    copies = []
    for k in range(chunks):
        part = pl.ds(k * count, count)
        copies.append(pltpu.make_async_copy(ref.at[part], buffer.at[part], sems.at[k]))
        copies[-1].start()
    return copies


def restrict_kernel(pos, owner, agg, r_ref, w_ref, *refs):
    out_refs, (acc, buffer, sems) = refs[:6], refs[6:]
    blocks_x, blocks_y = buffer.shape[:2]
    copies = started(r_ref, buffer, sems, blocks_x)
    acc[...] = jnp.zeros_like(acc)
    for p in range(blocks_x):
        copies[p].wait()
        for b in range(blocks_y):
            side = owner[p, b] - pos[1] + 1
            slot = agg[p, b] - pos[0] + 1
            acc[side, slot] += w_ref[p, b][None, :] * buffer[p, b]
    rows = out_refs[0].shape[2]
    for k, (side, flip) in enumerate(
        ((pos[4], 1 - pos[3]), (1, pos[3]), (2 - pos[4], 1 - pos[3]))
    ):
        for j, chip in enumerate((pos[5], 1 - pos[5])):
            for core in range(2):
                at = pl.multiple_of(quarter(flip, chip, core) * rows, rows)
                out_refs[2 * k + j][core] = acc[side, :, pl.ds(at, rows)]


def gather_kernel(pos, pair_s, own_s, next_s, pair_x, own_x, next_x, keep, send):
    core = pos[2]
    for k, refs in enumerate(((pair_s, own_s, next_s), (pair_x, own_x, next_x))):
        for out, c in ((keep, core), (send, 1 - core)):
            out[k] = refs[0][c] + refs[1][c] + refs[2][c]


def device_at(pos, k, sibling):
    chip = pos[5] if k == 0 else 1 - pos[5]
    return 2 * chip + (1 - pos[2] if sibling else pos[2])


def put_faces(s, last, pos, row_ref, inner, outer, y_pair, y_next):
    per, blocks_y = row_ref.shape[:2]
    core = pos[2]
    pair_side = jnp.where(pos[4] == 2, blocks_y - 1, 0)
    for t in range(per):
        y_pair[t] = row_ref[t, pair_side]
        y_next[t] = row_ref[t, blocks_y - 1 - pair_side]

    for end, row, lower in ((0, 0, 1), (last, per - 1, 0)):

        @pl.when((s == end) & (core == lower))
        def _():
            inner[...] = row_ref[row]

        @pl.when((s == end) & (core == 1 - lower))
        def _():
            outer[...] = row_ref[row]


def sweep_kernel(pos, r_ref, s_ref, f_ref, inner, outer, y_pair, y_next):
    s = pl.program_id(0)
    per, blocks_y = r_ref.shape[:2]
    for t in range(per):
        for b in range(blocks_y):
            f_ref[t, b] = product(r_ref[t, b], s_ref[t, b])
    put_faces(s, pl.num_programs(0) - 1, pos, f_ref, inner, outer, y_pair, y_next)


def neighbours_off(result, face, before, after, left, right):
    result = result - face[0][None, :] * before
    result = result - face[1][None, :] * after
    result = result - face[2][None, :] * left
    return result - face[3][None, :] * right


def fine_kernel(
    pos,
    r_ref,
    s_ref,
    diag_ref,
    face_ref,
    v_ref,
    x_inner,
    x_outer,
    y_pair,
    y_next,
    out_ref,
    before,
    after,
):
    s = pl.program_id(0)
    last = pl.num_programs(0) - 1
    per, blocks_y = r_ref.shape[:2]

    @pl.when((s == 0) & (pos[2] == 0))
    def _():
        before[...] = x_outer[...]

    @pl.when((s == 0) & (pos[2] == 1))
    def _():
        before[...] = x_inner[...]

    @pl.when(s > 0)
    def _():
        before[...] = v_ref[jnp.maximum(s * per - 1, 0)]

    @pl.when((s == last) & (pos[2] == 0))
    def _():
        after[...] = x_inner[...]

    @pl.when((s == last) & (pos[2] == 1))
    def _():
        after[...] = x_outer[...]

    @pl.when(s < last)
    def _():
        after[...] = v_ref[jnp.minimum((s + 1) * per, v_ref.shape[0] - 1)]

    even = pos[4] == 2

    def low_side(t):
        return jnp.where(even, y_next[t], y_pair[t])

    def high_side(t):
        return jnp.where(even, y_pair[t], y_next[t])

    for t in range(per):
        p = s * per + t
        for b in range(blocks_y):
            here = v_ref[p, b]
            image = neighbours_off(
                product(here, diag_ref[t, b]),
                face_ref[t, b],
                before[b] if t == 0 else v_ref[p - 1, b],
                after[b] if t == per - 1 else v_ref[p + 1, b],
                low_side(t) if b == 0 else v_ref[p, b - 1],
                high_side(t) if b == blocks_y - 1 else v_ref[p, b + 1],
            )
            out_ref[t, b] = here + product(r_ref[t, b] - image, s_ref[t, b])


def coarse_first_kernel(pos, keep, other, smooth_ref, rhs_ref, first_ref, sums, buffer, sems):
    parts = sums.shape[0]
    share = sums.shape[1] - 2
    copies = started(smooth_ref, buffer, sems, parts)
    for k in range(2):
        sums[device_at(pos, k, False)] = keep[k]
        sums[device_at(pos, k, True)] = other[k]
    for part in range(parts):
        copies[part].wait()
        for i in range(share):
            value = sums[part, i + 1]
            if i == 0 and part > 0:
                value = value + sums[part - 1, share + 1]
            if i == share - 1 and part < parts - 1:
                value = value + sums[part + 1, 0]
            a = part * share + i
            rhs_ref[a] = value
            first_ref[a] = product(value, buffer[a])


def coarse_own_kernel(rhs_ref, first_ref, diag_ref, out_ref, buffer, sems):
    parts = sems.shape[0]
    share = buffer.shape[0] // parts
    copies = started(diag_ref, buffer, sems, parts)
    for part in range(parts):
        copies[part].wait()
        for a in range(part * share, (part + 1) * share):
            out_ref[a] = rhs_ref[a] - product(first_ref[a], buffer[a])


def coarse_last_kernel(
    pos,
    nbr,
    inner_ref,
    pair_ref,
    first_ref,
    next_ref,
    smooth_ref,
    weight_ref,
    keep,
    send,
    slab,
    window,
    buffer,
    sems,
    window_sems,
):
    parts, slots = slab.shape[:2]
    share = slots - 2
    total = window.shape[0] // 3
    copies = started(smooth_ref, buffer, sems, parts)
    moves = []
    for k, (side, ref) in enumerate(((pos[4], pair_ref), (1, first_ref), (2 - pos[4], next_ref))):
        target = window.at[pl.ds(pl.multiple_of(side * total, total), total)]
        moves.append(pltpu.make_async_copy(ref, target, window_sems.at[k]))
        moves[-1].start()
    slab[0, 0] = jnp.zeros_like(inner_ref[0])
    slab[parts - 1, share + 1] = jnp.zeros_like(inner_ref[0])
    for move in moves:
        move.wait()
    for part in range(parts):
        copies[part].wait()
        for i in range(share):
            a = part * share + i
            value = inner_ref[a]
            for n in range(weight_ref.shape[1]):
                at = nbr[a, n] - (pos[1] - 1) * total
                value = value + weight_ref[a, n][None, :] * window[at]
            value = first_ref[a] + product(value, buffer[a])
            slab[part, i + 1] = value
            if i == 0 and part > 0:
                slab[part - 1, share + 1] = value
            if i == share - 1 and part < parts - 1:
                slab[part + 1, 0] = value
    for k in range(2):
        keep[k] = slab[device_at(pos, k, False)]
        send[k] = slab[device_at(pos, k, True)]


def fill_table(pos, refs, table):
    rows = refs[0].shape[2]
    for k, (side, flip) in enumerate(
        ((pos[4], 1 - pos[3]), (1, pos[3]), (2 - pos[4], 1 - pos[3]))
    ):
        for j, chip in enumerate((pos[5], 1 - pos[5])):
            for c, core in enumerate((pos[2], 1 - pos[2])):
                at = pl.multiple_of(quarter(flip, chip, core) * rows, rows)
                table[side, :, pl.ds(at, rows)] = refs[2 * k + j][c]


def corrected(pos, owner, agg, table, fine, weight, p, b):
    side = owner[p, b] - pos[1] + 1
    slot = agg[p, b] - pos[0] + 1
    return fine + weight[None, :] * table[side, slot]


def rim_kernel(
    pos, owner, agg, fine_ref, w_ref, *refs
):
    messages, (y_pair, y_next, table, col_buf, sems) = refs[:6], refs[6:]
    blocks_x, blocks_y = w_ref.shape[:2]
    copies = []
    for k in range(2):
        source = fine_ref.at[:, k * (blocks_y - 1)]
        copies.append(pltpu.make_async_copy(source, col_buf.at[k], sems.at[k]))
        copies[-1].start()
    fill_table(pos, messages, table)
    for copy in copies:
        copy.wait()
    pair_at = jnp.where(pos[4] == 2, 1, 0)
    for at, ref in ((1 - pair_at, y_next), (pair_at, y_pair)):
        q = at * (blocks_y - 1)
        for p in range(blocks_x):
            ref[p] = corrected(pos, owner, agg, table, col_buf[at, p], w_ref[p, q], p, q)


def finish_kernel(
    pos,
    owner,
    agg,
    fine_ref,
    w_ref,
    r_ref,
    diag_ref,
    face_ref,
    *refs,
):
    messages, (out_ref, res_ref, inner, outer, table, solved) = refs[:6], refs[6:]
    s = pl.program_id(0)
    last = pl.num_programs(0) - 1
    per, blocks_y = fine_ref.shape[:2]
    blocks_x = solved.shape[0] - 2

    @pl.when(s == 0)
    def _():
        fill_table(pos, messages, table)
        solved[0] = jnp.zeros_like(solved[0])
        solved[blocks_x + 1] = jnp.zeros_like(solved[0])

    @pl.when(s < last)
    def _():
        for t in range(per):
            p = s * per + t
            for b in range(blocks_y):
                value = corrected(pos, owner, agg, table, fine_ref[t, b], w_ref[t, b], p, b)
                solved[p + 1, b] = value
                out_ref[t, b] = value
        for end, row, lower in ((0, 0, 1), (last - 1, per - 1, 0)):

            @pl.when((s == end) & (pos[2] == lower))
            def _():
                inner[...] = out_ref[row]

            @pl.when((s == end) & (pos[2] == 1 - lower))
            def _():
                outer[...] = out_ref[row]

    @pl.when(s > 0)
    def _():
        for t in range(per):
            p = (s - 1) * per + t
            for b in range(blocks_y):
                face = face_ref[t, b]
                value = r_ref[t, b] - product(solved[p + 1, b], diag_ref[t, b])
                value = value + face[0][None, :] * solved[p, b]
                value = value + face[1][None, :] * solved[p + 2, b]
                if b > 0:
                    value = value + face[2][None, :] * solved[p + 1, b - 1]
                if b < blocks_y - 1:
                    value = value + face[3][None, :] * solved[p + 1, b + 1]
                res_ref[t, b] = value


def border_kernel(
    pos, part_ref, face_ref, x_inner, x_outer, y_pair, y_next, out_ref, row_buf, col_buf, sems
):
    blocks_x, blocks_y = face_ref.shape[:2]
    core = pos[2]
    ends = (0, blocks_x - 1)
    sides = (0, blocks_y - 1)
    inside = pl.ds(1, blocks_x - 2)
    pairs = [(out_ref.at[p], row_buf.at[k]) for k, p in enumerate(ends)]
    pairs += [(out_ref.at[inside, q], col_buf.at[k]) for k, q in enumerate(sides)]
    loads = [pltpu.make_async_copy(a, b, sems.at[k]) for k, (a, b) in enumerate(pairs)]
    for load in loads:
        load.start()
    for load in loads:
        load.wait()
    for k, p in enumerate(ends):
        lower = core == k
        for b in range(blocks_y):
            beyond = jnp.where(lower, x_outer[b], x_inner[b])
            row_buf[k, b] += face_ref[p, b, k][None, :] * beyond
    even = pos[4] == 2
    for k, q in enumerate(sides):
        from_pair = even if k == 1 else jnp.logical_not(even)

        def beyond_y(p):
            return jnp.where(from_pair, y_pair[p], y_next[p])

        for j, p in enumerate(ends):
            row_buf[j, q] += face_ref[p, q, 2 + k][None, :] * beyond_y(p)
        for p in range(1, blocks_x - 1):
            col_buf[k, p - 1] += face_ref[p, q, 2 + k][None, :] * beyond_y(p)
    stores = [pltpu.make_async_copy(b, a, sems.at[4 + k]) for k, (a, b) in enumerate(pairs)]
    for store in stores:
        store.start()
    for store in stores:
        store.wait()


def to_sibling(array):
    return moved_to(array, lambda x, y: (x ^ 1, y))


def x_halo(inner, outer):
    return to_sibling(inner), moved_to(outer, lambda x, y: (((x + 1) ^ 1) - 1, y))


def y_halo(y_pair, y_next):
    return in_pair(y_pair), between_pairs(y_next)


def body(
    right_side,
    diag_blocks,
    smoother,
    face_weight,
    restrict_weight,
    prolong_weight,
    block_owner,
    block_aggregate,
    coarse_diag,
    coarse_smooth,
    neighbors,
    neighbor_weight,
):
    blocks_x, blocks_y, rows, size = right_side.shape
    total = coarse_diag.shape[0]
    parts = lax.axis_size("gx")
    share = total // parts
    per = 2
    steps = blocks_x // per
    fine_shape = right_side.shape
    mat_shape = diag_blocks.shape
    slab = (parts, share + 2, rows // parts, size)
    message = (2,) + slab[1:]
    coarse_shape = (total, rows // parts, size)
    x_face = (blocks_y, rows, size)
    y_face = (blocks_x, rows, size)
    block_flops = 2 * 4 * rows * size * size
    fine_count = blocks_x * blocks_y
    fine_bytes = fine_count * rows * size * 4
    coarse_flops = total * block_flops // parts
    coarse_bytes = total * size * size * 4
    hbm = pl.BlockSpec(memory_space=pl.ANY)
    fine_block = part_block(fine_shape, per)
    mat_block = part_block(mat_shape, per)
    weight_block = part_block(face_weight.shape, per)
    vmem = pl.BlockSpec(memory_space=pltpu.VMEM)
    cmat_scratch = [
        pltpu.VMEM(coarse_diag.shape, F32),
        pltpu.SemaphoreType.DMA((parts,)),
    ]
    face_specs = [whole(x_face)] * 2 + [part_block(y_face, per)] * 2
    face_shapes = [like(x_face)] * 2 + [like(y_face)] * 2

    gx, gy = lax.axis_index("gx"), lax.axis_index("gy")
    pos = jnp.stack([gx * share, gy, gx % 2, gy % 2, 2 * (1 - gy % 2), gx // 2]).astype(jnp.int32)

    pair_s, pair_x, own_s, own_x, next_s, next_x = call(
        restrict_kernel,
        1,
        [hbm, whole(restrict_weight.shape)],
        [vmem] * 6,
        [like(message)] * 6,
        scalars=3,
        scratch=[
            pltpu.VMEM((3, share + 2, rows, size), F32),
            pltpu.VMEM(fine_shape, F32),
            pltpu.SemaphoreType.DMA((blocks_x,)),
        ],
        moved=2 * fine_bytes,
    )(pos, block_owner, block_aggregate, right_side, restrict_weight)

    sums = (
        in_pair(pair_s),
        own_s,
        between_pairs(next_s),
        in_pair_crossed(pair_x),
        to_partner(own_x),
        between_pairs_crossed(next_x),
    )

    sweep, *faces = call(
        sweep_kernel,
        steps,
        [fine_block, mat_block],
        [fine_block] + face_specs,
        [like(fine_shape)] + face_shapes,
        scalars=1,
        flops=fine_count * block_flops,
        moved=3 * fine_bytes,
    )(pos, right_side, smoother)

    sums, sweep = lax.optimization_barrier((sums, sweep))
    keep, send = call(
        gather_kernel,
        1,
        [vmem] * 6,
        [vmem] * 2,
        [like(message)] * 2,
        scalars=1,
        moved=coarse_bytes,
    )(pos, *sums)
    other, sweep_x = lax.optimization_barrier((to_sibling(send), x_halo(*faces[:2])))

    rhs, first = call(
        coarse_first_kernel,
        1,
        [vmem, vmem, hbm],
        [vmem] * 2,
        [like(coarse_shape)] * 2,
        scalars=1,
        scratch=[pltpu.VMEM(slab, F32)] + cmat_scratch,
        flops=coarse_flops,
        moved=coarse_bytes,
    )(pos, keep, other, coarse_smooth)

    first, rhs, y_faces = lax.optimization_barrier((first, rhs, faces[2:]))
    sweep_y = y_halo(*y_faces)
    pair_first = in_pair_crossed(first)
    next_first = between_pairs_crossed(first)

    inner = call(
        coarse_own_kernel,
        1,
        [vmem, vmem, hbm],
        vmem,
        like(coarse_shape),
        scratch=cmat_scratch,
        flops=coarse_flops,
        moved=coarse_bytes,
    )(rhs, first, coarse_diag)

    keep, send = call(
        coarse_last_kernel,
        1,
        [vmem] * 4 + [hbm, vmem],
        [vmem] * 2,
        [like(message)] * 2,
        scalars=2,
        scratch=[pltpu.VMEM(slab, F32), pltpu.VMEM((3 * total,) + coarse_shape[1:], F32)]
        + cmat_scratch
        + [pltpu.SemaphoreType.DMA((3,))],
        flops=coarse_flops,
        moved=coarse_bytes,
    )(pos, neighbors, inner, pair_first, first, next_first, coarse_smooth, neighbor_weight)

    send, sweep_y = lax.optimization_barrier((send, sweep_y))
    other = to_sibling(send)
    mine = jnp.stack([keep[0], other[0]])
    partners = jnp.stack([keep[1], other[1]])
    tables = (
        in_pair(mine),
        in_pair_crossed(partners),
        mine,
        to_partner(partners),
        between_pairs(mine),
        between_pairs_crossed(partners),
    )

    fine_part = call(
        fine_kernel,
        steps,
        [fine_block] + [mat_block] * 2 + [weight_block, whole(fine_shape)]
        + [whole(x_face)] * 2
        + [part_block(y_face, per)] * 2,
        fine_block,
        like(fine_shape),
        scalars=1,
        scratch=[pltpu.VMEM(x_face, F32)] * 2,
        flops=2 * fine_count * block_flops,
        moved=5 * fine_bytes,
    )(pos, right_side, smoother, diag_blocks, face_weight, sweep, *sweep_x, *sweep_y)

    rim = call(
        rim_kernel,
        1,
        [hbm, whole(prolong_weight.shape)] + [vmem] * 6,
        [vmem] * 2,
        [like(y_face)] * 2,
        scalars=3,
        scratch=[
            pltpu.VMEM((3, share + 2, rows, size), F32),
            pltpu.VMEM((2,) + y_face, F32),
            pltpu.SemaphoreType.DMA((2,)),
        ],
        moved=fine_bytes,
    )(pos, block_owner, block_aggregate, fine_part, prolong_weight, *tables)
    solved_y = y_halo(*rim)

    def now(shape):
        return pl.BlockSpec(
            (per,) + tuple(shape[1:]),
            lambda s, *_: (jnp.minimum(s, steps - 1),) + (0,) * (len(shape) - 1),
        )

    def previous(shape):
        return pl.BlockSpec(
            (per,) + tuple(shape[1:]),
            lambda s, *_: (jnp.maximum(s - 1, 0),) + (0,) * (len(shape) - 1),
        )

    solved, residual, *x_faces = call(
        finish_kernel,
        steps + 1,
        [
            now(fine_shape),
            now(prolong_weight.shape),
            previous(fine_shape),
            previous(mat_shape),
            previous(face_weight.shape),
        ]
        + [vmem] * 6,
        [now(fine_shape), previous(fine_shape)] + [vmem] * 2,
        [like(fine_shape)] * 2 + [like(x_face)] * 2,
        scalars=3,
        scratch=[
            pltpu.VMEM((3, share + 2, rows, size), F32),
            pltpu.VMEM((blocks_x + 2, blocks_y, rows, size), F32),
        ],
        flops=fine_count * block_flops,
        moved=5 * fine_bytes,
    )(
        pos,
        block_owner,
        block_aggregate,
        fine_part,
        prolong_weight,
        right_side,
        diag_blocks,
        face_weight,
        *tables,
    )

    residual = call(
        border_kernel,
        1,
        [hbm, whole(face_weight.shape)] + [vmem] * 4,
        hbm,
        like(fine_shape),
        scalars=1,
        scratch=[
            pltpu.VMEM((2,) + x_face, F32),
            pltpu.VMEM((2, blocks_x - 2, rows, size), F32),
            pltpu.SemaphoreType.DMA((8,)),
        ],
        moved=fine_bytes,
        aliases={1: 0},
    )(pos, residual, face_weight, *x_halo(*x_faces), *solved_y)
    return (solved, residual)


def solution(mesh):
    return jax.shard_map(
        body,
        mesh=mesh,
        in_specs=(
            P("gx", "gy", None, None),
            P("gx", "gy", None, None),
            P("gx", "gy", None, None),
            P("gx", "gy", None, None),
            P("gx", "gy", None),
            P("gx", "gy", None),
            P("gx", "gy"),
            P("gx", "gy"),
            P("gy", None, None),
            P("gy", None, None),
            P("gy", None),
            P("gy", None, None),
        ),
        out_specs=(P("gx", "gy", None, None), P("gx", "gy", None, None)),
        check_vma=False,
    )
```

```python
import functools

import jax
import jax.numpy as jnp
from jax import lax
from jax.experimental import pallas as pl
from jax.experimental.pallas import tpu as pltpu
from jax.sharding import PartitionSpec as P

F32 = jnp.float32
BF16 = jnp.bfloat16


def moved_to(array, target):
    count_x, count_y = lax.axis_size("gx"), lax.axis_size("gy")
    pairs = []
    for x in range(count_x):
        for y in range(count_y):
            to_x, to_y = target(x, y)
            if 0 <= to_x < count_x and 0 <= to_y < count_y:
                pairs.append((x * count_y + y, to_x * count_y + to_y))
    return lax.ppermute(array, ("gx", "gy"), pairs)


def in_pair(array):
    return moved_to(array, lambda x, y: (x, y ^ 1))


def in_pair_crossed(array):
    return moved_to(array, lambda x, y: (x ^ 2, y ^ 1))


def between_pairs(array):
    return moved_to(array, lambda x, y: (x, ((y + 1) ^ 1) - 1))


def between_pairs_crossed(array):
    return moved_to(array, lambda x, y: (x ^ 2, ((y + 1) ^ 1) - 1))


def to_partner(array):
    return moved_to(array, lambda x, y: (x ^ 2, y))


def quarter(flip, chip, core):
    return 2 * jnp.where(flip == 1, 1 - chip, chip) + core


def halves(x):
    high = x.astype(BF16)
    low = (x - high.astype(F32)).astype(BF16)
    return high, low


def product(vector, matrix):
    vector_high, vector_low = halves(vector)
    matrix_high, matrix_low = halves(matrix)
    left = jnp.concatenate([vector_high, vector_low], axis=1)
    right = jnp.concatenate(
        [
            jnp.concatenate([matrix_high, matrix_high], axis=1),
            jnp.concatenate([matrix_low, matrix_low], axis=1),
        ],
        axis=0,
    )
    both = lax.dot_general(left, right, (((1,), (1,)), ((), ())), preferred_element_type=F32)
    width = matrix.shape[0]
    return both[:, :width] + both[:, width:]


def call(kernel, grid, in_specs, out_specs, out_shape, scalars=0, scratch=(), flops=0, moved=0, aliases=None, limit=32):
    return pl.pallas_call(
        kernel,
        grid_spec=pltpu.PrefetchScalarGridSpec(
            num_scalar_prefetch=scalars,
            grid=(grid,),
            in_specs=in_specs,
            out_specs=out_specs,
            scratch_shapes=list(scratch),
        ),
        out_shape=out_shape,
        input_output_aliases=aliases or {},
        compiler_params=pltpu.CompilerParams(vmem_limit_bytes=limit * 1024 * 1024),
        cost_estimate=pl.CostEstimate(flops=40 * flops, bytes_accessed=40 * moved, transcendentals=0),
    )


def part_block(shape, count):
    return pl.BlockSpec((count,) + tuple(shape[1:]), lambda s, *_: (s,) + (0,) * (len(shape) - 1))


def whole(shape):
    return pl.BlockSpec(tuple(shape), lambda s, *_: (0,) * len(shape))


def like(shape):
    return jax.ShapeDtypeStruct(tuple(shape), F32)


def started(ref, buffer, sems, chunks):
    count = buffer.shape[0] // chunks
    copies = []
    for k in range(chunks):
        part = pl.ds(k * count, count)
        copies.append(pltpu.make_async_copy(ref.at[part], buffer.at[part], sems.at[k]))
        copies[-1].start()
    return copies


def restrict_kernel(pos, owner, agg, r_ref, w_ref, *refs):
    out_refs, (acc, buffer, sems) = refs[:6], refs[6:]
    blocks_x, blocks_y = buffer.shape[:2]
    copies = started(r_ref, buffer, sems, blocks_x)
    acc[...] = jnp.zeros_like(acc)
    for p in range(blocks_x):
        copies[p].wait()
        for b in range(blocks_y):
            side = owner[p, b] - pos[1] + 1
            slot = agg[p, b] - pos[0] + 1
            acc[side, slot] += w_ref[p, b][None, :] * buffer[p, b]
    rows = out_refs[0].shape[2]
    for k, (side, flip) in enumerate(
        ((pos[4], 1 - pos[3]), (1, pos[3]), (2 - pos[4], 1 - pos[3]))
    ):
        for j, chip in enumerate((pos[5], 1 - pos[5])):
            for core in range(2):
                at = pl.multiple_of(quarter(flip, chip, core) * rows, rows)
                out_refs[2 * k + j][core] = acc[side, :, pl.ds(at, rows)]


def gather_kernel(pos, pair_s, next_x, pair_x, next_s, own_x, own_s, keep, send):
    core = pos[2]
    for k, refs in enumerate(((pair_s, own_s, next_s), (pair_x, own_x, next_x))):
        for out, c in ((keep, core), (send, 1 - core)):
            out[k] = refs[0][c] + refs[1][c] + refs[2][c]


def device_at(pos, k, sibling):
    chip = pos[5] if k == 0 else 1 - pos[5]
    return 2 * chip + (1 - pos[2] if sibling else pos[2])


def put_faces(s, last, pos, row_ref, inner, outer, y_pair, y_next):
    per, blocks_y = row_ref.shape[:2]
    core = pos[2]
    pair_side = jnp.where(pos[4] == 2, blocks_y - 1, 0)
    for t in range(per):
        y_pair[t] = row_ref[t, pair_side]
        y_next[t] = row_ref[t, blocks_y - 1 - pair_side]

    for end, row, lower in ((0, 0, 1), (last, per - 1, 0)):

        @pl.when((s == end) & (core == lower))
        def _():
            inner[...] = row_ref[row]

        @pl.when((s == end) & (core == 1 - lower))
        def _():
            outer[...] = row_ref[row]


def sweep_kernel(pos, r_ref, s_ref, f_ref, inner, outer, y_pair, y_next):
    s = pl.program_id(0)
    per, blocks_y = r_ref.shape[:2]
    for t in range(per):
        for b in range(blocks_y):
            f_ref[t, b] = product(r_ref[t, b], s_ref[t, b])
    put_faces(s, pl.num_programs(0) - 1, pos, f_ref, inner, outer, y_pair, y_next)


def neighbours_off(result, face, before, after, left, right):
    result = result - face[0][None, :] * before
    result = result - face[1][None, :] * after
    result = result - face[2][None, :] * left
    return result - face[3][None, :] * right


def fine_kernel(
    pos,
    r_ref,
    s_ref,
    diag_ref,
    face_ref,
    v_ref,
    x_inner,
    x_outer,
    y_pair,
    y_next,
    out_ref,
    before,
    after,
):
    s = pl.program_id(0)
    last = pl.num_programs(0) - 1
    per, blocks_y = r_ref.shape[:2]

    @pl.when((s == 0) & (pos[2] == 0))
    def _():
        before[...] = x_outer[...]

    @pl.when((s == 0) & (pos[2] == 1))
    def _():
        before[...] = x_inner[...]

    @pl.when(s > 0)
    def _():
        before[...] = v_ref[jnp.maximum(s * per - 1, 0)]

    @pl.when((s == last) & (pos[2] == 0))
    def _():
        after[...] = x_inner[...]

    @pl.when((s == last) & (pos[2] == 1))
    def _():
        after[...] = x_outer[...]

    @pl.when(s < last)
    def _():
        after[...] = v_ref[jnp.minimum((s + 1) * per, v_ref.shape[0] - 1)]

    even = pos[4] == 2

    def low_side(t):
        return jnp.where(even, y_next[t], y_pair[t])

    def high_side(t):
        return jnp.where(even, y_pair[t], y_next[t])

    for t in range(per):
        p = s * per + t
        for b in range(blocks_y):
            here = v_ref[p, b]
            image = neighbours_off(
                product(here, diag_ref[t, b]),
                face_ref[t, b],
                before[b] if t == 0 else v_ref[p - 1, b],
                after[b] if t == per - 1 else v_ref[p + 1, b],
                low_side(t) if b == 0 else v_ref[p, b - 1],
                high_side(t) if b == blocks_y - 1 else v_ref[p, b + 1],
            )
            out_ref[t, b] = here + product(r_ref[t, b] - image, s_ref[t, b])


def coarse_first_kernel(pos, keep, other, smooth_ref, rhs_ref, first_ref, sums, buffer, sems):
    parts = sums.shape[0]
    share = sums.shape[1] - 2
    copies = started(smooth_ref, buffer, sems, parts)
    for k in range(2):
        sums[device_at(pos, k, False)] = keep[k]
        sums[device_at(pos, k, True)] = other[k]
    for part in range(parts):
        copies[part].wait()
        for i in range(share):
            value = sums[part, i + 1]
            if i == 0 and part > 0:
                value = value + sums[part - 1, share + 1]
            if i == share - 1 and part < parts - 1:
                value = value + sums[part + 1, 0]
            a = part * share + i
            rhs_ref[a] = value
            first_ref[a] = product(value, buffer[a])


def coarse_own_kernel(rhs_ref, first_ref, diag_ref, out_ref, buffer, sems):
    parts = sems.shape[0]
    share = buffer.shape[0] // parts
    copies = started(diag_ref, buffer, sems, parts)
    for part in range(parts):
        copies[part].wait()
        for a in range(part * share, (part + 1) * share):
            out_ref[a] = rhs_ref[a] - product(first_ref[a], buffer[a])


def coarse_last_kernel(
    pos,
    nbr,
    inner_ref,
    pair_ref,
    first_ref,
    next_ref,
    smooth_ref,
    weight_ref,
    keep,
    send,
    slab,
    window,
    buffer,
    sems,
    window_sems,
):
    parts, slots = slab.shape[:2]
    share = slots - 2
    total = window.shape[0] // 3
    copies = started(smooth_ref, buffer, sems, parts)
    moves = []
    for k, (side, ref) in enumerate(((pos[4], pair_ref), (1, first_ref), (2 - pos[4], next_ref))):
        target = window.at[pl.ds(pl.multiple_of(side * total, total), total)]
        moves.append(pltpu.make_async_copy(ref, target, window_sems.at[k]))
        moves[-1].start()
    slab[0, 0] = jnp.zeros_like(inner_ref[0])
    slab[parts - 1, share + 1] = jnp.zeros_like(inner_ref[0])
    for move in moves:
        move.wait()
    for part in range(parts):
        copies[part].wait()
        for i in range(share):
            a = part * share + i
            value = inner_ref[a]
            for n in range(weight_ref.shape[1]):
                at = nbr[a, n] - (pos[1] - 1) * total
                value = value + weight_ref[a, n][None, :] * window[at]
            value = first_ref[a] + product(value, buffer[a])
            slab[part, i + 1] = value
            if i == 0 and part > 0:
                slab[part - 1, share + 1] = value
            if i == share - 1 and part < parts - 1:
                slab[part + 1, 0] = value
    for k in range(2):
        keep[k] = slab[device_at(pos, k, False)]
        send[k] = slab[device_at(pos, k, True)]


def fill_table(pos, refs, table):
    pair_s, next_x, pair_x, next_s, own_x, own_s = refs
    refs = (pair_s, pair_x, own_s, own_x, next_s, next_x)
    rows = own_s.shape[2]
    for k, (side, flip) in enumerate(
        ((pos[4], 1 - pos[3]), (1, pos[3]), (2 - pos[4], 1 - pos[3]))
    ):
        for j, chip in enumerate((pos[5], 1 - pos[5])):
            for c, core in enumerate((pos[2], 1 - pos[2])):
                at = pl.multiple_of(quarter(flip, chip, core) * rows, rows)
                table[side, :, pl.ds(at, rows)] = refs[2 * k + j][c]


def corrected(pos, owner, agg, table, fine, weight, p, b):
    side = owner[p, b] - pos[1] + 1
    slot = agg[p, b] - pos[0] + 1
    return fine + weight[None, :] * table[side, slot]


def rim_kernel(
    pos, owner, agg, fine_ref, w_ref, *refs
):
    messages, (y_pair, y_next, table, col_buf, sems) = refs[:6], refs[6:]
    blocks_x, blocks_y = w_ref.shape[:2]
    copies = []
    for k in range(2):
        source = fine_ref.at[:, k * (blocks_y - 1)]
        copies.append(pltpu.make_async_copy(source, col_buf.at[k], sems.at[k]))
        copies[-1].start()
    fill_table(pos, messages, table)
    for copy in copies:
        copy.wait()
    pair_at = jnp.where(pos[4] == 2, 1, 0)
    for at, ref in ((1 - pair_at, y_next), (pair_at, y_pair)):
        q = at * (blocks_y - 1)
        for p in range(blocks_x):
            ref[p] = corrected(pos, owner, agg, table, col_buf[at, p], w_ref[p, q], p, q)


def finish_kernel(
    pos,
    owner,
    agg,
    fine_ref,
    w_ref,
    r_ref,
    diag_ref,
    face_ref,
    *refs,
):
    messages, (out_ref, res_ref, inner, outer, table, solved) = refs[:6], refs[6:]
    s = pl.program_id(0)
    last = pl.num_programs(0) - 1
    per, blocks_y = fine_ref.shape[:2]
    blocks_x = solved.shape[0] - 2

    @pl.when(s == 0)
    def _():
        fill_table(pos, messages, table)
        solved[0] = jnp.zeros_like(solved[0])
        solved[blocks_x + 1] = jnp.zeros_like(solved[0])

    @pl.when(s < last)
    def _():
        for t in range(per):
            p = s * per + t
            for b in range(blocks_y):
                value = corrected(pos, owner, agg, table, fine_ref[t, b], w_ref[t, b], p, b)
                solved[p + 1, b] = value
                out_ref[t, b] = value
        for end, row, lower in ((0, 0, 1), (last - 1, per - 1, 0)):

            @pl.when((s == end) & (pos[2] == lower))
            def _():
                inner[...] = out_ref[row]

            @pl.when((s == end) & (pos[2] == 1 - lower))
            def _():
                outer[...] = out_ref[row]

    @pl.when(s > 0)
    def _():
        for t in range(per):
            p = (s - 1) * per + t
            for b in range(blocks_y):
                face = face_ref[t, b]
                value = r_ref[t, b] - product(solved[p + 1, b], diag_ref[t, b])
                value = value + face[0][None, :] * solved[p, b]
                value = value + face[1][None, :] * solved[p + 2, b]
                if b > 0:
                    value = value + face[2][None, :] * solved[p + 1, b - 1]
                if b < blocks_y - 1:
                    value = value + face[3][None, :] * solved[p + 1, b + 1]
                res_ref[t, b] = value


def updated(out_ref, views, buffer, sems, change):
    loads = [pltpu.make_async_copy(v, buffer.at[k], sems.at[k]) for k, v in enumerate(views)]
    for load in loads:
        load.start()
    stores = []
    for k, view in enumerate(views):
        loads[k].wait()
        for j in range(buffer.shape[1]):
            buffer[k, j] += change(k, j)
        stores.append(pltpu.make_async_copy(buffer.at[k], view, sems.at[2 + k]))
        stores[-1].start()
    for store in stores:
        store.wait()


def y_border_kernel(pos, part_ref, face_ref, y_pair, y_next, out_ref, buffer, sems):
    blocks_y = face_ref.shape[1]
    even = pos[4] == 2

    def change(k, p):
        from_pair = even if k == 1 else jnp.logical_not(even)
        beyond = jnp.where(from_pair, y_pair[p], y_next[p])
        return face_ref[p, k * (blocks_y - 1), 2 + k][None, :] * beyond

    views = [out_ref.at[:, k * (blocks_y - 1)] for k in range(2)]
    updated(out_ref, views, buffer, sems, change)


def x_border_kernel(pos, part_ref, face_ref, x_inner, x_outer, out_ref, buffer, sems):
    blocks_x = face_ref.shape[0]

    def change(k, b):
        beyond = jnp.where(pos[2] == k, x_outer[b], x_inner[b])
        return face_ref[k * (blocks_x - 1), b, k][None, :] * beyond

    views = [out_ref.at[k * (blocks_x - 1)] for k in range(2)]
    updated(out_ref, views, buffer, sems, change)


def to_sibling(array):
    return moved_to(array, lambda x, y: (x ^ 1, y))


def x_halo(inner, outer):
    return to_sibling(inner), moved_to(outer, lambda x, y: (((x + 1) ^ 1) - 1, y))


def y_halo(y_pair, y_next):
    return in_pair(y_pair), between_pairs(y_next)


def body(
    right_side,
    diag_blocks,
    smoother,
    face_weight,
    restrict_weight,
    prolong_weight,
    block_owner,
    block_aggregate,
    coarse_diag,
    coarse_smooth,
    neighbors,
    neighbor_weight,
):
    blocks_x, blocks_y, rows, size = right_side.shape
    total = coarse_diag.shape[0]
    parts = lax.axis_size("gx")
    share = total // parts
    per = 2
    steps = blocks_x // per
    fine_shape = right_side.shape
    mat_shape = diag_blocks.shape
    slab = (parts, share + 2, rows // parts, size)
    message = (2,) + slab[1:]
    coarse_shape = (total, rows // parts, size)
    x_face = (blocks_y, rows, size)
    y_face = (blocks_x, rows, size)
    block_flops = 2 * 4 * rows * size * size
    fine_count = blocks_x * blocks_y
    fine_bytes = fine_count * rows * size * 4
    coarse_flops = total * block_flops // parts
    coarse_bytes = total * size * size * 4
    hbm = pl.BlockSpec(memory_space=pl.ANY)
    fine_block = part_block(fine_shape, per)
    mat_block = part_block(mat_shape, per)
    weight_block = part_block(face_weight.shape, per)
    vmem = pl.BlockSpec(memory_space=pltpu.VMEM)
    cmat_scratch = [
        pltpu.VMEM(coarse_diag.shape, F32),
        pltpu.SemaphoreType.DMA((parts,)),
    ]
    face_specs = [whole(x_face)] * 2 + [part_block(y_face, per)] * 2
    face_shapes = [like(x_face)] * 2 + [like(y_face)] * 2

    gx, gy = lax.axis_index("gx"), lax.axis_index("gy")
    pos = jnp.stack([gx * share, gy, gx % 2, gy % 2, 2 * (1 - gy % 2), gx // 2]).astype(jnp.int32)

    pair_s, pair_x, own_s, own_x, next_s, next_x = call(
        restrict_kernel,
        1,
        [hbm, whole(restrict_weight.shape)],
        [vmem] * 6,
        [like(message)] * 6,
        scalars=3,
        scratch=[
            pltpu.VMEM((3, share + 2, rows, size), F32),
            pltpu.VMEM(fine_shape, F32),
            pltpu.SemaphoreType.DMA((blocks_x,)),
        ],
        moved=2 * fine_bytes,
    )(pos, block_owner, block_aggregate, right_side, restrict_weight)

    sums = (
        in_pair(pair_s),
        between_pairs_crossed(next_x),
        in_pair_crossed(pair_x),
        between_pairs(next_s),
        to_partner(own_x),
        own_s,
    )

    sweep, *faces = call(
        sweep_kernel,
        steps,
        [fine_block, mat_block],
        [fine_block] + face_specs,
        [like(fine_shape)] + face_shapes,
        scalars=1,
        flops=fine_count * block_flops,
        moved=3 * fine_bytes,
    )(pos, right_side, smoother)

    sums, sweep = lax.optimization_barrier((sums, sweep))
    keep, send = call(
        gather_kernel,
        1,
        [vmem] * 6,
        [vmem] * 2,
        [like(message)] * 2,
        scalars=1,
        moved=coarse_bytes,
    )(pos, *sums)
    other, sweep_x = lax.optimization_barrier((to_sibling(send), x_halo(*faces[:2])))

    rhs, first = call(
        coarse_first_kernel,
        1,
        [vmem, vmem, hbm],
        [vmem] * 2,
        [like(coarse_shape)] * 2,
        scalars=1,
        scratch=[pltpu.VMEM(slab, F32)] + cmat_scratch,
        flops=coarse_flops,
        moved=coarse_bytes,
    )(pos, keep, other, coarse_smooth)

    first, rhs, y_faces = lax.optimization_barrier((first, rhs, faces[2:]))
    sweep_y = y_halo(*y_faces)
    pair_first = in_pair_crossed(first)
    next_first = between_pairs_crossed(first)

    inner = call(
        coarse_own_kernel,
        1,
        [vmem, vmem, hbm],
        vmem,
        like(coarse_shape),
        scratch=cmat_scratch,
        flops=coarse_flops,
        moved=coarse_bytes,
    )(rhs, first, coarse_diag)

    keep, send = call(
        coarse_last_kernel,
        1,
        [vmem] * 4 + [hbm, vmem],
        [vmem] * 2,
        [like(message)] * 2,
        scalars=2,
        scratch=[pltpu.VMEM(slab, F32), pltpu.VMEM((3 * total,) + coarse_shape[1:], F32)]
        + cmat_scratch
        + [pltpu.SemaphoreType.DMA((3,))],
        flops=coarse_flops,
        moved=coarse_bytes,
    )(pos, neighbors, inner, pair_first, first, next_first, coarse_smooth, neighbor_weight)

    send, sweep_y = lax.optimization_barrier((send, sweep_y))
    other = to_sibling(send)
    mine = jnp.stack([keep[0], other[0]])
    partners = jnp.stack([keep[1], other[1]])
    tables = (
        in_pair(mine),
        between_pairs_crossed(partners),
        in_pair_crossed(partners),
        between_pairs(mine),
        to_partner(partners),
        mine,
    )

    fine_part = call(
        fine_kernel,
        steps,
        [fine_block] + [mat_block] * 2 + [weight_block, whole(fine_shape)]
        + [whole(x_face)] * 2
        + [part_block(y_face, per)] * 2,
        fine_block,
        like(fine_shape),
        scalars=1,
        scratch=[pltpu.VMEM(x_face, F32)] * 2,
        flops=2 * fine_count * block_flops,
        moved=5 * fine_bytes,
    )(pos, right_side, smoother, diag_blocks, face_weight, sweep, *sweep_x, *sweep_y)

    rim = call(
        rim_kernel,
        1,
        [hbm, whole(prolong_weight.shape)] + [vmem] * 6,
        [vmem] * 2,
        [like(y_face)] * 2,
        scalars=3,
        scratch=[
            pltpu.VMEM((3, share + 2, rows, size), F32),
            pltpu.VMEM((2,) + y_face, F32),
            pltpu.SemaphoreType.DMA((2,)),
        ],
        moved=fine_bytes,
    )(pos, block_owner, block_aggregate, fine_part, prolong_weight, *tables)
    solved_y = y_halo(*rim)

    def now(shape):
        return pl.BlockSpec(
            (per,) + tuple(shape[1:]),
            lambda s, *_: (jnp.minimum(s, steps - 1),) + (0,) * (len(shape) - 1),
        )

    def previous(shape):
        return pl.BlockSpec(
            (per,) + tuple(shape[1:]),
            lambda s, *_: (jnp.maximum(s - 1, 0),) + (0,) * (len(shape) - 1),
        )

    solved, residual, *x_faces = call(
        finish_kernel,
        steps + 1,
        [
            now(fine_shape),
            now(prolong_weight.shape),
            previous(fine_shape),
            previous(mat_shape),
            previous(face_weight.shape),
        ]
        + [vmem] * 6,
        [now(fine_shape), previous(fine_shape)] + [vmem] * 2,
        [like(fine_shape)] * 2 + [like(x_face)] * 2,
        scalars=3,
        scratch=[
            pltpu.VMEM((3, share + 2, rows, size), F32),
            pltpu.VMEM((blocks_x + 2, blocks_y, rows, size), F32),
        ],
        flops=fine_count * block_flops,
        moved=5 * fine_bytes,
    )(
        pos,
        block_owner,
        block_aggregate,
        fine_part,
        prolong_weight,
        right_side,
        diag_blocks,
        face_weight,
        *tables,
    )

    for kernel, face, beyond in (
        (y_border_kernel, y_face, solved_y),
        (x_border_kernel, x_face, x_halo(*x_faces)),
    ):
        residual = call(
            kernel,
            1,
            [hbm, whole(face_weight.shape)] + [vmem] * 2,
            hbm,
            like(fine_shape),
            scalars=1,
            scratch=[pltpu.VMEM((2,) + face, F32), pltpu.SemaphoreType.DMA((4,))],
            moved=fine_bytes,
            aliases={1: 0},
        )(pos, residual, face_weight, *beyond)
    return (solved, residual)


def solution(mesh):
    return jax.shard_map(
        body,
        mesh=mesh,
        in_specs=(
            P("gx", "gy", None, None),
            P("gx", "gy", None, None),
            P("gx", "gy", None, None),
            P("gx", "gy", None, None),
            P("gx", "gy", None),
            P("gx", "gy", None),
            P("gx", "gy"),
            P("gx", "gy"),
            P("gy", None, None),
            P("gy", None, None),
            P("gy", None),
            P("gy", None, None),
        ),
        out_specs=(P("gx", "gy", None, None), P("gx", "gy", None, None)),
        check_vma=False,
    )
```

```python
import functools

import jax
import jax.numpy as jnp
from jax import lax
from jax.experimental import pallas as pl
from jax.experimental.pallas import tpu as pltpu
from jax.sharding import PartitionSpec as P

F32 = jnp.float32
BF16 = jnp.bfloat16


def moved_to(array, target):
    count_x, count_y = lax.axis_size("gx"), lax.axis_size("gy")
    pairs = []
    for x in range(count_x):
        for y in range(count_y):
            to_x, to_y = target(x, y)
            if 0 <= to_x < count_x and 0 <= to_y < count_y:
                pairs.append((x * count_y + y, to_x * count_y + to_y))
    return lax.ppermute(array, ("gx", "gy"), pairs)


def in_pair(array):
    return moved_to(array, lambda x, y: (x, y ^ 1))


def in_pair_crossed(array):
    return moved_to(array, lambda x, y: (x ^ 2, y ^ 1))


def between_pairs(array):
    return moved_to(array, lambda x, y: (x, ((y + 1) ^ 1) - 1))


def between_pairs_crossed(array):
    return moved_to(array, lambda x, y: (x ^ 2, ((y + 1) ^ 1) - 1))


def to_partner(array):
    return moved_to(array, lambda x, y: (x ^ 2, y))


def quarter(flip, chip, core):
    return 2 * jnp.where(flip == 1, 1 - chip, chip) + core


def halves(x):
    high = x.astype(BF16)
    low = (x - high.astype(F32)).astype(BF16)
    return high, low


def product(vector, matrix):
    vector_high, vector_low = halves(vector)
    matrix_high, matrix_low = halves(matrix)
    left = jnp.concatenate([vector_high, vector_low], axis=1)
    right = jnp.concatenate(
        [
            jnp.concatenate([matrix_high, matrix_high], axis=1),
            jnp.concatenate([matrix_low, matrix_low], axis=1),
        ],
        axis=0,
    )
    both = lax.dot_general(left, right, (((1,), (1,)), ((), ())), preferred_element_type=F32)
    width = matrix.shape[0]
    return both[:, :width] + both[:, width:]


def call(kernel, grid, in_specs, out_specs, out_shape, scalars=0, scratch=(), flops=0, moved=0, aliases=None, limit=32):
    return pl.pallas_call(
        kernel,
        grid_spec=pltpu.PrefetchScalarGridSpec(
            num_scalar_prefetch=scalars,
            grid=(grid,),
            in_specs=in_specs,
            out_specs=out_specs,
            scratch_shapes=list(scratch),
        ),
        out_shape=out_shape,
        input_output_aliases=aliases or {},
        compiler_params=pltpu.CompilerParams(vmem_limit_bytes=limit * 1024 * 1024),
        cost_estimate=pl.CostEstimate(flops=40 * flops, bytes_accessed=40 * moved, transcendentals=0),
    )


def part_block(shape, count):
    return pl.BlockSpec((count,) + tuple(shape[1:]), lambda s, *_: (s,) + (0,) * (len(shape) - 1))


def whole(shape):
    return pl.BlockSpec(tuple(shape), lambda s, *_: (0,) * len(shape))


def like(shape):
    return jax.ShapeDtypeStruct(tuple(shape), F32)


def started(ref, buffer, sems, chunks):
    count = buffer.shape[0] // chunks
    copies = []
    for k in range(chunks):
        part = pl.ds(k * count, count)
        copies.append(pltpu.make_async_copy(ref.at[part], buffer.at[part], sems.at[k]))
        copies[-1].start()
    return copies


def restrict_kernel(pos, owner, agg, r_ref, w_ref, *refs):
    out_refs, (acc, buffer, sems) = refs[:6], refs[6:]
    blocks_x, blocks_y = buffer.shape[:2]
    copies = started(r_ref, buffer, sems, blocks_x)
    acc[...] = jnp.zeros_like(acc)
    for p in range(blocks_x):
        copies[p].wait()
        for b in range(blocks_y):
            side = owner[p, b] - pos[1] + 1
            slot = agg[p, b] - pos[0] + 1
            acc[side, slot] += w_ref[p, b][None, :] * buffer[p, b]
    rows = out_refs[0].shape[2]
    for k, (side, flip) in enumerate(
        ((pos[4], 1 - pos[3]), (1, pos[3]), (2 - pos[4], 1 - pos[3]))
    ):
        for j, chip in enumerate((pos[5], 1 - pos[5])):
            for core in range(2):
                at = pl.multiple_of(quarter(flip, chip, core) * rows, rows)
                out_refs[2 * k + j][core] = acc[side, :, pl.ds(at, rows)]


def gather_kernel(pos, pair_s, next_x, pair_x, next_s, own_x, own_s, keep, send):
    core = pos[2]
    for k, refs in enumerate(((pair_s, own_s, next_s), (pair_x, own_x, next_x))):
        for out, c in ((keep, core), (send, 1 - core)):
            out[k] = refs[0][c] + refs[1][c] + refs[2][c]


def device_at(pos, k, sibling):
    chip = pos[5] if k == 0 else 1 - pos[5]
    return 2 * chip + (1 - pos[2] if sibling else pos[2])


def put_faces(s, last, pos, row_ref, inner, outer, y_pair, y_next):
    per, blocks_y = row_ref.shape[:2]
    core = pos[2]
    pair_side = jnp.where(pos[4] == 2, blocks_y - 1, 0)
    for t in range(per):
        y_pair[t] = row_ref[t, pair_side]
        y_next[t] = row_ref[t, blocks_y - 1 - pair_side]

    for end, row, lower in ((0, 0, 1), (last, per - 1, 0)):

        @pl.when((s == end) & (core == lower))
        def _():
            inner[...] = row_ref[row]

        @pl.when((s == end) & (core == 1 - lower))
        def _():
            outer[...] = row_ref[row]


def sweep_kernel(pos, r_ref, s_ref, f_ref, inner, outer, y_pair, y_next):
    s = pl.program_id(0)
    per, blocks_y = r_ref.shape[:2]
    for t in range(per):
        for b in range(blocks_y):
            f_ref[t, b] = product(r_ref[t, b], s_ref[t, b])
    put_faces(s, pl.num_programs(0) - 1, pos, f_ref, inner, outer, y_pair, y_next)


def neighbours_off(result, face, before, after, left, right):
    result = result - face[0][None, :] * before
    result = result - face[1][None, :] * after
    result = result - face[2][None, :] * left
    return result - face[3][None, :] * right


def fine_kernel(
    pos,
    r_ref,
    s_ref,
    diag_ref,
    face_ref,
    v_ref,
    x_inner,
    x_outer,
    y_pair,
    y_next,
    out_ref,
    before,
    after,
):
    s = pl.program_id(0)
    last = pl.num_programs(0) - 1
    per, blocks_y = r_ref.shape[:2]

    @pl.when((s == 0) & (pos[2] == 0))
    def _():
        before[...] = x_outer[...]

    @pl.when((s == 0) & (pos[2] == 1))
    def _():
        before[...] = x_inner[...]

    @pl.when(s > 0)
    def _():
        before[...] = v_ref[jnp.maximum(s * per - 1, 0)]

    @pl.when((s == last) & (pos[2] == 0))
    def _():
        after[...] = x_inner[...]

    @pl.when((s == last) & (pos[2] == 1))
    def _():
        after[...] = x_outer[...]

    @pl.when(s < last)
    def _():
        after[...] = v_ref[jnp.minimum((s + 1) * per, v_ref.shape[0] - 1)]

    even = pos[4] == 2

    def low_side(t):
        return jnp.where(even, y_next[t], y_pair[t])

    def high_side(t):
        return jnp.where(even, y_pair[t], y_next[t])

    for t in range(per):
        p = s * per + t
        for b in range(blocks_y):
            here = v_ref[p, b]
            image = neighbours_off(
                product(here, diag_ref[t, b]),
                face_ref[t, b],
                before[b] if t == 0 else v_ref[p - 1, b],
                after[b] if t == per - 1 else v_ref[p + 1, b],
                low_side(t) if b == 0 else v_ref[p, b - 1],
                high_side(t) if b == blocks_y - 1 else v_ref[p, b + 1],
            )
            out_ref[t, b] = here + product(r_ref[t, b] - image, s_ref[t, b])


def coarse_first_kernel(pos, keep, other, smooth_ref, rhs_ref, first_ref, sums, buffer, sems):
    parts = sums.shape[0]
    share = sums.shape[1] - 2
    copies = started(smooth_ref, buffer, sems, parts)
    for k in range(2):
        sums[device_at(pos, k, False)] = keep[k]
        sums[device_at(pos, k, True)] = other[k]
    for part in range(parts):
        copies[part].wait()
        for i in range(share):
            value = sums[part, i + 1]
            if i == 0 and part > 0:
                value = value + sums[part - 1, share + 1]
            if i == share - 1 and part < parts - 1:
                value = value + sums[part + 1, 0]
            a = part * share + i
            rhs_ref[a] = value
            first_ref[a] = product(value, buffer[a])


def coarse_own_kernel(rhs_ref, first_ref, diag_ref, out_ref, buffer, sems):
    parts = sems.shape[0]
    share = buffer.shape[0] // parts
    copies = started(diag_ref, buffer, sems, parts)
    for part in range(parts):
        copies[part].wait()
        for a in range(part * share, (part + 1) * share):
            out_ref[a] = rhs_ref[a] - product(first_ref[a], buffer[a])


def coarse_last_kernel(
    pos,
    nbr,
    inner_ref,
    pair_ref,
    first_ref,
    next_ref,
    smooth_ref,
    weight_ref,
    keep,
    send,
    slab,
    window,
    buffer,
    sems,
    window_sems,
):
    parts, slots = slab.shape[:2]
    share = slots - 2
    total = window.shape[0] // 3
    copies = started(smooth_ref, buffer, sems, parts)
    moves = []
    for k, (side, ref) in enumerate(((pos[4], pair_ref), (1, first_ref), (2 - pos[4], next_ref))):
        target = window.at[pl.ds(pl.multiple_of(side * total, total), total)]
        moves.append(pltpu.make_async_copy(ref, target, window_sems.at[k]))
        moves[-1].start()
    slab[0, 0] = jnp.zeros_like(inner_ref[0])
    slab[parts - 1, share + 1] = jnp.zeros_like(inner_ref[0])
    for move in moves:
        move.wait()
    for part in range(parts):
        copies[part].wait()
        for i in range(share):
            a = part * share + i
            value = inner_ref[a]
            for n in range(weight_ref.shape[1]):
                at = nbr[a, n] - (pos[1] - 1) * total
                value = value + weight_ref[a, n][None, :] * window[at]
            value = first_ref[a] + product(value, buffer[a])
            slab[part, i + 1] = value
            if i == 0 and part > 0:
                slab[part - 1, share + 1] = value
            if i == share - 1 and part < parts - 1:
                slab[part + 1, 0] = value
    for k in range(2):
        keep[k] = slab[device_at(pos, k, False)]
        send[k] = slab[device_at(pos, k, True)]


def fill_table(pos, refs, table):
    pair_s, next_x, pair_x, next_s, own_x, own_s = refs
    refs = (pair_s, pair_x, own_s, own_x, next_s, next_x)
    rows = own_s.shape[2]
    for k, (side, flip) in enumerate(
        ((pos[4], 1 - pos[3]), (1, pos[3]), (2 - pos[4], 1 - pos[3]))
    ):
        for j, chip in enumerate((pos[5], 1 - pos[5])):
            for c, core in enumerate((pos[2], 1 - pos[2])):
                at = pl.multiple_of(quarter(flip, chip, core) * rows, rows)
                table[side, :, pl.ds(at, rows)] = refs[2 * k + j][c]


def corrected(pos, owner, agg, table, fine, weight, p, b):
    side = owner[p, b] - pos[1] + 1
    slot = agg[p, b] - pos[0] + 1
    return fine + weight[None, :] * table[side, slot]


def rim_kernel(
    pos, owner, agg, fine_ref, w_ref, *refs
):
    messages, (y_pair, y_next, table, col_buf, sems) = refs[:6], refs[6:]
    blocks_x, blocks_y = w_ref.shape[:2]
    copies = []
    for k in range(2):
        source = fine_ref.at[:, k * (blocks_y - 1)]
        copies.append(pltpu.make_async_copy(source, col_buf.at[k], sems.at[k]))
        copies[-1].start()
    fill_table(pos, messages, table)
    for copy in copies:
        copy.wait()
    pair_at = jnp.where(pos[4] == 2, 1, 0)
    for at, ref in ((1 - pair_at, y_next), (pair_at, y_pair)):
        q = at * (blocks_y - 1)
        for p in range(blocks_x):
            ref[p] = corrected(pos, owner, agg, table, col_buf[at, p], w_ref[p, q], p, q)


def finish_kernel(
    pos,
    owner,
    agg,
    fine_ref,
    w_ref,
    r_ref,
    diag_ref,
    face_ref,
    *refs,
):
    messages, (out_ref, res_ref, inner, outer, table, solved) = refs[:6], refs[6:]
    s = pl.program_id(0)
    last = pl.num_programs(0) - 1
    per, blocks_y = fine_ref.shape[:2]
    blocks_x = solved.shape[0] - 2

    @pl.when(s == 0)
    def _():
        fill_table(pos, messages, table)
        solved[0] = jnp.zeros_like(solved[0])
        solved[blocks_x + 1] = jnp.zeros_like(solved[0])

    @pl.when(s < last)
    def _():
        for t in range(per):
            p = s * per + t
            for b in range(blocks_y):
                value = corrected(pos, owner, agg, table, fine_ref[t, b], w_ref[t, b], p, b)
                solved[p + 1, b] = value
                out_ref[t, b] = value
        for end, row, lower in ((0, 0, 1), (last - 1, per - 1, 0)):

            @pl.when((s == end) & (pos[2] == lower))
            def _():
                inner[...] = out_ref[row]

            @pl.when((s == end) & (pos[2] == 1 - lower))
            def _():
                outer[...] = out_ref[row]

    @pl.when(s > 0)
    def _():
        for t in range(per):
            p = (s - 1) * per + t
            for b in range(blocks_y):
                face = face_ref[t, b]
                value = r_ref[t, b] - product(solved[p + 1, b], diag_ref[t, b])
                value = value + face[0][None, :] * solved[p, b]
                value = value + face[1][None, :] * solved[p + 2, b]
                if b > 0:
                    value = value + face[2][None, :] * solved[p + 1, b - 1]
                if b < blocks_y - 1:
                    value = value + face[3][None, :] * solved[p + 1, b + 1]
                res_ref[t, b] = value


def updated(out_ref, views, buffer, sems, change):
    loads = [pltpu.make_async_copy(v, buffer.at[k], sems.at[k]) for k, v in enumerate(views)]
    for load in loads:
        load.start()
    stores = []
    for k, view in enumerate(views):
        loads[k].wait()
        for j in range(buffer.shape[1]):
            buffer[k, j] += change(k, j)
        stores.append(pltpu.make_async_copy(buffer.at[k], view, sems.at[2 + k]))
        stores[-1].start()
    for store in stores:
        store.wait()


def y_border_kernel(pos, part_ref, face_ref, y_pair, y_next, out_ref, buffer, sems):
    blocks_y = face_ref.shape[1]
    even = pos[4] == 2

    def change(k, p):
        from_pair = even if k == 1 else jnp.logical_not(even)
        beyond = jnp.where(from_pair, y_pair[p], y_next[p])
        return face_ref[p, k * (blocks_y - 1), 2 + k][None, :] * beyond

    views = [out_ref.at[:, k * (blocks_y - 1)] for k in range(2)]
    updated(out_ref, views, buffer, sems, change)


def x_border_kernel(pos, part_ref, face_ref, x_inner, x_outer, out_ref, buffer, sems):
    blocks_x = face_ref.shape[0]

    def change(k, b):
        beyond = jnp.where(pos[2] == k, x_outer[b], x_inner[b])
        return face_ref[k * (blocks_x - 1), b, k][None, :] * beyond

    views = [out_ref.at[k * (blocks_x - 1)] for k in range(2)]
    updated(out_ref, views, buffer, sems, change)


def to_sibling(array):
    return moved_to(array, lambda x, y: (x ^ 1, y))


def x_halo(inner, outer):
    return to_sibling(inner), moved_to(outer, lambda x, y: (((x + 1) ^ 1) - 1, y))


def y_halo(y_pair, y_next):
    return in_pair(y_pair), between_pairs(y_next)


def body(
    right_side,
    diag_blocks,
    smoother,
    face_weight,
    restrict_weight,
    prolong_weight,
    block_owner,
    block_aggregate,
    coarse_diag,
    coarse_smooth,
    neighbors,
    neighbor_weight,
):
    blocks_x, blocks_y, rows, size = right_side.shape
    total = coarse_diag.shape[0]
    parts = lax.axis_size("gx")
    share = total // parts
    per = 2
    steps = blocks_x // per
    fine_shape = right_side.shape
    mat_shape = diag_blocks.shape
    slab = (parts, share + 2, rows // parts, size)
    message = (2,) + slab[1:]
    coarse_shape = (total, rows // parts, size)
    x_face = (blocks_y, rows, size)
    y_face = (blocks_x, rows, size)
    block_flops = 2 * 4 * rows * size * size
    fine_count = blocks_x * blocks_y
    fine_bytes = fine_count * rows * size * 4
    coarse_flops = total * block_flops // parts
    coarse_bytes = total * size * size * 4
    hbm = pl.BlockSpec(memory_space=pl.ANY)
    fine_block = part_block(fine_shape, per)
    mat_block = part_block(mat_shape, per)
    weight_block = part_block(face_weight.shape, per)
    vmem = pl.BlockSpec(memory_space=pltpu.VMEM)
    cmat_scratch = [
        pltpu.VMEM(coarse_diag.shape, F32),
        pltpu.SemaphoreType.DMA((parts,)),
    ]
    face_specs = [whole(x_face)] * 2 + [part_block(y_face, per)] * 2
    face_shapes = [like(x_face)] * 2 + [like(y_face)] * 2

    gx, gy = lax.axis_index("gx"), lax.axis_index("gy")
    pos = jnp.stack([gx * share, gy, gx % 2, gy % 2, 2 * (1 - gy % 2), gx // 2]).astype(jnp.int32)

    pair_s, pair_x, own_s, own_x, next_s, next_x = call(
        restrict_kernel,
        1,
        [hbm, whole(restrict_weight.shape)],
        [vmem] * 6,
        [like(message)] * 6,
        scalars=3,
        scratch=[
            pltpu.VMEM((3, share + 2, rows, size), F32),
            pltpu.VMEM(fine_shape, F32),
            pltpu.SemaphoreType.DMA((blocks_x,)),
        ],
        moved=2 * fine_bytes,
        limit=60,
    )(pos, block_owner, block_aggregate, right_side, restrict_weight)

    sums = (
        in_pair(pair_s),
        between_pairs_crossed(next_x),
        in_pair_crossed(pair_x),
        between_pairs(next_s),
        to_partner(own_x),
        own_s,
    )

    sweep, *faces = call(
        sweep_kernel,
        steps,
        [fine_block, mat_block],
        [fine_block] + face_specs,
        [like(fine_shape)] + face_shapes,
        scalars=1,
        flops=fine_count * block_flops,
        moved=3 * fine_bytes,
    )(pos, right_side, smoother)

    sums, sweep = lax.optimization_barrier((sums, sweep))
    keep, send = call(
        gather_kernel,
        1,
        [vmem] * 6,
        [vmem] * 2,
        [like(message)] * 2,
        scalars=1,
        moved=coarse_bytes,
    )(pos, *sums)
    other, sweep_x = lax.optimization_barrier((to_sibling(send), x_halo(*faces[:2])))

    rhs, first = call(
        coarse_first_kernel,
        1,
        [vmem, vmem, hbm],
        [whole(coarse_shape), vmem],
        [like(coarse_shape)] * 2,
        scalars=1,
        scratch=[pltpu.VMEM(slab, F32)] + cmat_scratch,
        flops=coarse_flops,
        moved=coarse_bytes,
    )(pos, keep, other, coarse_smooth)

    first, rhs, y_faces = lax.optimization_barrier((first, rhs, faces[2:]))
    sweep_y = y_halo(*y_faces)
    pair_first = in_pair_crossed(first)
    next_first = between_pairs_crossed(first)

    inner = call(
        coarse_own_kernel,
        1,
        [whole(coarse_shape), vmem, hbm],
        vmem,
        like(coarse_shape),
        scratch=cmat_scratch,
        flops=coarse_flops,
        moved=coarse_bytes,
    )(rhs, first, coarse_diag)

    keep, send = call(
        coarse_last_kernel,
        1,
        [vmem] * 4 + [hbm, vmem],
        [vmem] * 2,
        [like(message)] * 2,
        scalars=2,
        scratch=[pltpu.VMEM(slab, F32), pltpu.VMEM((3 * total,) + coarse_shape[1:], F32)]
        + cmat_scratch
        + [pltpu.SemaphoreType.DMA((3,))],
        flops=coarse_flops,
        moved=coarse_bytes,
    )(pos, neighbors, inner, pair_first, first, next_first, coarse_smooth, neighbor_weight)

    send, sweep_y = lax.optimization_barrier((send, sweep_y))
    other = to_sibling(send)
    mine = jnp.stack([keep[0], other[0]])
    partners = jnp.stack([keep[1], other[1]])
    tables = (
        in_pair(mine),
        between_pairs_crossed(partners),
        in_pair_crossed(partners),
        between_pairs(mine),
        to_partner(partners),
        mine,
    )

    fine_part = call(
        fine_kernel,
        steps,
        [fine_block] + [mat_block] * 2 + [weight_block, whole(fine_shape)]
        + [whole(x_face)] * 2
        + [part_block(y_face, per)] * 2,
        fine_block,
        like(fine_shape),
        scalars=1,
        scratch=[pltpu.VMEM(x_face, F32)] * 2,
        flops=2 * fine_count * block_flops,
        moved=5 * fine_bytes,
    )(pos, right_side, smoother, diag_blocks, face_weight, sweep, *sweep_x, *sweep_y)

    rim = call(
        rim_kernel,
        1,
        [hbm, whole(prolong_weight.shape)] + [vmem] * 6,
        [vmem] * 2,
        [like(y_face)] * 2,
        scalars=3,
        scratch=[
            pltpu.VMEM((3, share + 2, rows, size), F32),
            pltpu.VMEM((2,) + y_face, F32),
            pltpu.SemaphoreType.DMA((2,)),
        ],
        moved=fine_bytes,
    )(pos, block_owner, block_aggregate, fine_part, prolong_weight, *tables)
    solved_y = y_halo(*rim)

    def now(shape):
        return pl.BlockSpec(
            (per,) + tuple(shape[1:]),
            lambda s, *_: (jnp.minimum(s, steps - 1),) + (0,) * (len(shape) - 1),
        )

    def previous(shape):
        return pl.BlockSpec(
            (per,) + tuple(shape[1:]),
            lambda s, *_: (jnp.maximum(s - 1, 0),) + (0,) * (len(shape) - 1),
        )

    solved, residual, *x_faces = call(
        finish_kernel,
        steps + 1,
        [
            now(fine_shape),
            now(prolong_weight.shape),
            previous(fine_shape),
            previous(mat_shape),
            previous(face_weight.shape),
        ]
        + [vmem] * 6,
        [now(fine_shape), previous(fine_shape)] + [vmem] * 2,
        [like(fine_shape)] * 2 + [like(x_face)] * 2,
        scalars=3,
        scratch=[
            pltpu.VMEM((3, share + 2, rows, size), F32),
            pltpu.VMEM((blocks_x + 2, blocks_y, rows, size), F32),
        ],
        flops=fine_count * block_flops,
        moved=5 * fine_bytes,
    )(
        pos,
        block_owner,
        block_aggregate,
        fine_part,
        prolong_weight,
        right_side,
        diag_blocks,
        face_weight,
        *tables,
    )

    for kernel, face, beyond in (
        (y_border_kernel, y_face, solved_y),
        (x_border_kernel, x_face, x_halo(*x_faces)),
    ):
        residual = call(
            kernel,
            1,
            [hbm, whole(face_weight.shape)] + [vmem] * 2,
            hbm,
            like(fine_shape),
            scalars=1,
            scratch=[pltpu.VMEM((2,) + face, F32), pltpu.SemaphoreType.DMA((4,))],
            moved=fine_bytes,
            aliases={1: 0},
        )(pos, residual, face_weight, *beyond)
    return (solved, residual)


def solution(mesh):
    return jax.shard_map(
        body,
        mesh=mesh,
        in_specs=(
            P("gx", "gy", None, None),
            P("gx", "gy", None, None),
            P("gx", "gy", None, None),
            P("gx", "gy", None, None),
            P("gx", "gy", None),
            P("gx", "gy", None),
            P("gx", "gy"),
            P("gx", "gy"),
            P("gy", None, None),
            P("gy", None, None),
            P("gy", None),
            P("gy", None, None),
        ),
        out_specs=(P("gx", "gy", None, None), P("gx", "gy", None, None)),
        check_vma=False,
    )
```
